256 devices in a mesh: pipe: 8 (over x, core), expert: 32 (over y, z).
Axes of the slice: x: 4, y: 4, z: 8, core: 2. Of those that a mesh axis runs over, the one named last changes fastest.
Arguments:
- upper_grad: bfloat16 [1024, 6144], P('expert', 'pipe'), may hold values from -6 to 6
- expert_ids: int32 [1024, 4], P('expert'), may hold values from 0 to 7, as said below
- slot_index: int32 [1024, 4], P('expert'), may hold values from -1 to 23, as said below
- gate_probs: float32 [1024, 4], P('expert'), may hold values from 0.05 to 0.6
- gate_pre: bfloat16 [32, 768, 1344], P('expert'), may hold values from -6 to 6
- up_pre: bfloat16 [32, 768, 1344], P('expert'), may hold values from -6 to 6
- w_gate: bfloat16 [32, 6144, 1344], P('expert', 'pipe'), may hold values from -0.078125 to 0.078125
- w_up: bfloat16 [32, 6144, 1344], P('expert', 'pipe'), may hold values from -0.078125 to 0.078125
- w_down: bfloat16 [32, 1344, 6144], P('expert', None, 'pipe'), may hold values from -0.078125 to 0.078125
- query_heads: bfloat16 [4096, 6144], P('expert', 'pipe'), may hold values from -6 to 6
- key_heads: bfloat16 [4096, 1024], P('expert', 'pipe'), may hold values from -6 to 6
- value_heads: bfloat16 [4096, 1024], P('expert', 'pipe'), may hold values from -6 to 6
- attn_out: bfloat16 [4096, 6144], P('expert', 'pipe'), may hold values from -4 to 4
- head_grad: bfloat16 [4096, 6144], P('expert', 'pipe'), may hold values from -6 to 6
Outputs:
- moe_input_grad: bfloat16 [1024, 6144], P('expert', 'pipe')
- query_grad: bfloat16 [4096, 6144], P('expert', 'pipe')
- key_grad: bfloat16 [4096, 1024], P('expert', 'pipe')
- value_grad: bfloat16 [4096, 1024], P('expert', 'pipe')
The draws below stay inside these ranges and needn't reach their ends.
Inputs may be any that keep to these rules, and one draw needn't show every extreme that they name: `expert_ids`: each token names 4 different experts; one expert is named by every token. `slot_index`: within the 32 tokens of one index of expert, a pair's slot is its rank among that index's pairs to the same expert in order of token then choice, or -1 once that rank reaches 24; so at most 24 slots from one index to one expert, and some expert receives 24 from every index.
All inputs are finite; a program needn't handle non-finite values.
Results may differ from the reference program's by a relative error of at most 0.019.
Values may be sent and summed in bfloat16 or wider, within the bound.
A program may use at most 64 MiB of HBM per device.

```python
import jax
import jax.numpy as jnp
from jax import lax

D = 6144
EXPERTS = 8
EXPERT_UNITS = 5376
TOP = 4
HEAD_DIM = 128
KV_HEADS = 8
GROUP = 6
TOK = 32
ATT_TOK = 128
UNITS_GROUP = 1344
TOKENS = 1024
ATT_TOKENS = 4096
CAP = 24
SLOTS = 768
Q_WIDTH = 6144
KV_WIDTH = 1024
N_EXPERT = 32


def routing_tables(key):
    expert_iota = jnp.arange(EXPERTS, dtype=jnp.int32)
    scores = jax.random.randint(key, (TOKENS, EXPERTS), 0, 1 << 20)
    favour = jax.random.randint(jax.random.fold_in(key, 9), (1, EXPERTS), 0, 1 << 19)
    hottest = jax.random.randint(jax.random.fold_in(key, 7), (1, 1), 0, EXPERTS)
    scores = scores + favour + jnp.where(expert_iota == hottest, 1 << 22, 0)
    scores = scores * EXPERTS + expert_iota
    unused, chosen = lax.top_k(scores, TOP)
    chosen = chosen.astype(jnp.int32)
    pairs = chosen.reshape(N_EXPERT, TOK * TOP)
    onehot = (pairs[..., None] == expert_iota).astype(jnp.int32)
    ranked = jnp.sum((jnp.cumsum(onehot, axis=1) - 1) * onehot, axis=2)
    slotted = jnp.where(ranked < CAP, ranked, -1).astype(jnp.int32)
    return (chosen, slotted.reshape(TOKENS, TOP))


def draw_expert_ids(key, part):
    return routing_tables(key)[0]


def draw_slot_index(key, part):
    return routing_tables(key)[1]


def draw_query_heads(key, part):
    key = jax.random.fold_in(key, 11)
    shape = (ATT_TOKENS, KV_HEADS, GROUP, HEAD_DIM)
    drawn = jnp.clip(jax.random.normal(key, shape, jnp.float32), -4.0, 4.0)
    return drawn.reshape(ATT_TOKENS, KV_HEADS * GROUP * HEAD_DIM).astype(jnp.bfloat16)


def draw_key_heads(key, part):
    key = jax.random.fold_in(key, 13)
    shape = (ATT_TOKENS, KV_HEADS, HEAD_DIM)
    drawn = jnp.clip(jax.random.normal(key, shape, jnp.float32), -4.0, 4.0)
    return drawn.reshape(ATT_TOKENS, KV_HEADS * HEAD_DIM).astype(jnp.bfloat16)


def shard_levels(own_key, dims, cuts, low, high):
    gain = 1.0
    for dim, blocks in cuts:
        draws = jax.random.uniform(jax.random.fold_in(jax.random.fold_in(own_key, 6), dim), (blocks,), jnp.float32, low / len(cuts), high / len(cuts))
        gain = gain * jnp.repeat(jnp.exp(draws), dims[dim] // blocks).reshape((-1,) + (1,) * (len(dims) - 1 - dim))
    return gain


def scatter_about(key, extent, spread, limit, shards=(), held_as=jnp.bfloat16):
    loudness = shard_levels(key, extent, shards, -0.22, 0.18) if shards else 1.0
    values = jax.random.normal(key, extent, jnp.float32) * spread * loudness
    return jnp.minimum(jnp.maximum(values, -limit), limit).astype(held_as)


def setup_inputs(seed: int = 0) -> dict:
    key_of = jax.random.split(jax.random.key(seed), 15)
    return {
        "upper_grad": scatter_about(key_of[0], (TOKENS, D), 1.0, 6.0, ((0, 32), (1, 8))),
        "expert_ids": draw_expert_ids(jax.random.fold_in(key_of[14], 71), 0),
        "slot_index": draw_slot_index(jax.random.fold_in(key_of[14], 71), 0),
        "gate_probs": jnp.clip(0.05 + 0.55 * jax.random.uniform(key_of[3], (TOKENS, TOP), jnp.float32) ** shard_levels(key_of[3], (TOKENS, TOP), ((0, 32),), -0.2, 0.2), 0.05, 0.6),
        "gate_pre": scatter_about(key_of[4], (N_EXPERT, SLOTS, UNITS_GROUP), 1.0, 6.0, ((0, 32),)),
        "up_pre": scatter_about(key_of[5], (N_EXPERT, SLOTS, UNITS_GROUP), 1.0, 6.0, ((0, 32),)),
        "w_gate": scatter_about(key_of[6], (N_EXPERT, D, UNITS_GROUP), D ** -0.5, 0.078125, ((0, 32), (1, 8))),
        "w_up": scatter_about(key_of[7], (N_EXPERT, D, UNITS_GROUP), D ** -0.5, 0.078125, ((0, 32), (1, 8))),
        "w_down": scatter_about(key_of[8], (N_EXPERT, UNITS_GROUP, D), EXPERT_UNITS ** -0.5, 0.078125, ((0, 32), (2, 8))),
        "query_heads": draw_query_heads(jax.random.fold_in(key_of[14], 71), 0),
        "key_heads": draw_key_heads(jax.random.fold_in(key_of[14], 71), 0),
        "value_heads": scatter_about(key_of[11], (ATT_TOKENS, KV_WIDTH), 1.0, 6.0, ((0, 32), (1, 8))),
        "attn_out": scatter_about(key_of[12], (ATT_TOKENS, Q_WIDTH), 0.5, 4.0, ((0, 32), (1, 8))),
        "head_grad": scatter_about(key_of[13], (ATT_TOKENS, Q_WIDTH), 1.0, 6.0, ((0, 32), (1, 8))),
    }


masked_value = -1e30


def expert_backward(slot_rows, gate_in, up_in, gate_mat, up_mat, down_mat):
    gate_full = gate_in.transpose(1, 0, 2).reshape(SLOTS, EXPERT_UNITS)
    up_full = up_in.transpose(1, 0, 2).reshape(SLOTS, EXPERT_UNITS)
    gate_matrix = gate_mat.transpose(1, 0, 2).reshape(D, EXPERT_UNITS)
    up_matrix = up_mat.transpose(1, 0, 2).reshape(D, EXPERT_UNITS)
    down_matrix = down_mat.reshape(EXPERT_UNITS, D)
    hidden_grad = lax.dot_general(slot_rows, down_matrix, (((1,), (1,)), ((), ())), preferred_element_type=jnp.float32)
    gate_val = gate_full.astype(jnp.float32)
    up_val = up_full.astype(jnp.float32)
    sigmoid_val = jax.nn.sigmoid(gate_val)
    gate_grad = (hidden_grad * up_val * sigmoid_val * (1.0 + gate_val * (1.0 - sigmoid_val))).astype(jnp.bfloat16)
    up_grad = (hidden_grad * gate_val * sigmoid_val).astype(jnp.bfloat16)
    first_term = lax.dot_general(gate_grad, gate_matrix, (((1,), (1,)), ((), ())), preferred_element_type=jnp.float32)
    second_term = lax.dot_general(up_grad, up_matrix, (((1,), (1,)), ((), ())), preferred_element_type=jnp.float32)
    return first_term + second_term


def moe_reference(incoming, expert_ids, slot_index, gate_probs, gate_pre, up_pre, w_gate, w_up, w_down):
    group_devs = N_EXPERT // EXPERTS
    units_group = EXPERT_UNITS // group_devs
    source = (jnp.arange(TOKENS, dtype=jnp.int32) // TOK)[:, None]
    kept = slot_index >= 0
    place = jnp.where(kept, expert_ids * SLOTS + source * CAP + slot_index, EXPERTS * SLOTS).astype(jnp.int32)
    rows_out = (gate_probs[:, :, None] * incoming[:, None, :].astype(jnp.float32)).astype(jnp.bfloat16)
    buffer = jnp.zeros((EXPERTS * SLOTS + 1, D), jnp.bfloat16)
    buffer = buffer.at[place.reshape(-1)].set(rows_out.reshape(-1, D))
    buffer = buffer[:-1].reshape(EXPERTS, SLOTS, D)
    items = (buffer,
             gate_pre.reshape(EXPERTS, group_devs, SLOTS, units_group),
             up_pre.reshape(EXPERTS, group_devs, SLOTS, units_group),
             w_gate.reshape(EXPERTS, group_devs, D, units_group),
             w_up.reshape(EXPERTS, group_devs, D, units_group),
             w_down.reshape(EXPERTS, group_devs, units_group, D))
    returned = lax.map(lambda parts: expert_backward(*parts), items)
    returned = jnp.concatenate([returned.reshape(-1, D), jnp.zeros((1, D), jnp.float32)], axis=0)
    picked = returned[place]
    return (incoming.astype(jnp.float32) + jnp.sum(picked, axis=1)).astype(jnp.bfloat16)


def attention_reference(query_heads, key_heads, value_heads, attn_out, head_grad):
    softmax_scale = HEAD_DIM ** -0.5
    queries = query_heads.astype(jnp.float32).reshape(ATT_TOKENS, KV_HEADS, GROUP, HEAD_DIM)
    outputs = attn_out.astype(jnp.float32).reshape(ATT_TOKENS, KV_HEADS, GROUP, HEAD_DIM)
    grad_out = head_grad.astype(jnp.float32).reshape(ATT_TOKENS, KV_HEADS, GROUP, HEAD_DIM)
    key_all = key_heads.astype(jnp.float32).reshape(ATT_TOKENS, KV_HEADS, HEAD_DIM)
    value_all = value_heads.astype(jnp.float32).reshape(ATT_TOKENS, KV_HEADS, HEAD_DIM)
    key_acc = jnp.zeros((ATT_TOKENS, KV_HEADS, HEAD_DIM), jnp.float32)
    value_acc = jnp.zeros((ATT_TOKENS, KV_HEADS, HEAD_DIM), jnp.float32)
    query_parts = []
    for block_id in range(N_EXPERT):
        row_start = block_id * ATT_TOK
        row_end = row_start + ATT_TOK
        query_block = queries[row_start:row_end]
        out_block = outputs[row_start:row_end]
        grad_block = grad_out[row_start:row_end]
        key_block = key_all[:row_end]
        value_block = value_all[:row_end]
        scores = jnp.einsum('thgd,lhd->hgtl', query_block, key_block) * softmax_scale
        causal = jnp.arange(row_end)[None, :] <= (row_start + jnp.arange(ATT_TOK))[:, None]
        scores = jnp.where(causal, scores, masked_value)
        row_max = jnp.max(scores, axis=-1, keepdims=True)
        log_total = row_max + jnp.log(jnp.sum(jnp.exp(scores - row_max), axis=-1, keepdims=True))
        probs = jnp.exp(scores - log_total)
        probs_low = lax.optimization_barrier(probs.astype(jnp.bfloat16)).astype(jnp.float32)
        grad_probs = jnp.einsum('thgd,lhd->hgtl', grad_block, value_block)
        row_delta = jnp.einsum('thgd,thgd->hgt', grad_block, out_block)[..., None]
        grad_scores = (probs * (grad_probs - row_delta) * softmax_scale).astype(jnp.bfloat16)
        grad_scores = lax.optimization_barrier(grad_scores).astype(jnp.float32)
        query_parts.append(jnp.einsum('hgtl,lhd->thgd', grad_scores, key_block))
        key_part = jnp.einsum('hgtl,thgd->lhd', grad_scores, query_block).astype(jnp.bfloat16)
        value_part = jnp.einsum('hgtl,thgd->lhd', probs_low, grad_block).astype(jnp.bfloat16)
        key_acc = key_acc.at[:row_end].add(lax.optimization_barrier(key_part).astype(jnp.float32))
        value_acc = value_acc.at[:row_end].add(lax.optimization_barrier(value_part).astype(jnp.float32))
    query_grad = jnp.concatenate(query_parts, axis=0).reshape(ATT_TOKENS, Q_WIDTH).astype(jnp.bfloat16)
    key_grad = key_acc.reshape(ATT_TOKENS, KV_WIDTH).astype(jnp.bfloat16)
    value_grad = value_acc.reshape(ATT_TOKENS, KV_WIDTH).astype(jnp.bfloat16)
    return query_grad, key_grad, value_grad


def reference(upper_grad, expert_ids, slot_index, gate_probs, gate_pre, up_pre, w_gate, w_up, w_down, query_heads, key_heads, value_heads, attn_out, head_grad):
    moe_input_grad = moe_reference(upper_grad, expert_ids, slot_index, gate_probs, gate_pre, up_pre, w_gate, w_up, w_down)
    query_grad, key_grad, value_grad = attention_reference(query_heads, key_heads, value_heads, attn_out, head_grad)
    return (moe_input_grad, query_grad, key_grad, value_grad)
```

```python
import jax
import jax.numpy as jnp
from jax import lax
from jax.experimental import pallas as pl
from jax.experimental.pallas import tpu as pltpu
from jax.sharding import PartitionSpec as P

MESH = pl.DeviceIdType.MESH
F32 = jnp.float32
BF16 = jnp.bfloat16

EXPERTS = 8
HEAD_DIM = 128
GROUP = 6
TOK = 32
ATT = 128
CAP = 24
UNITS = 1344
COLS = 768
ROWS = GROUP * ATT
NX, NC, NY, NZ = 4, 2, 4, 8
PAIRS = NZ // 2
PAIR_SLOTS = 2 * CAP
ROW_SLOTS = NZ * CAP
HALF_SLOTS = ROW_SLOTS // 2
KEYS = 2 * ATT
BLOCKS = NY * PAIRS
SCALE = HEAD_DIM ** (-0.5)
MASKED = -1e30

NT = (((1,), (1,)), ((), ()))
TN = (((0,), (0,)), ((), ()))
NN = (((1,), (0,)), ((), ()))


def dot(a, b, dims):
    return lax.dot_general(a, b, dims, preferred_element_type=F32)


def kernel(
    upper_ref, ids_ref, slot_ref, prob_ref, gpre_hbm, upre_hbm, wg_hbm, wu_hbm, wd_hbm,
    q_ref, k_ref, v_ref, o_ref, do_ref,
    moe_ref, dq_ref, dk_ref, dv_ref,
    gpre, upre, wg, wu, wd, load_sem,
    upg, metag, stack, picks, tables, sbuf, arrived,
    hpart, csend, crecv, xsend, xrecv, hidg,
    tsend, trecv, zsend, zrecv, mown,
    kvg, qrows, dorows, delta, scores, mrun, lrun, dqt, dkv, drecv, dzsend, dzrecv, dtmp,
    up_s, up_r, meta_s, meta_r, kvz_s, kvz_r, kvy_s, kvy_r, sl_s, sl_r,
    core_s, core_r, xr_s, xr_r, xg_s, xg_r, cg_s, cg_r, t_s, t_r, tz_s, tz_r,
    dy_s, dy_r, dz_s, dz_r,
):
    p = lax.axis_index("pipe")
    e = lax.axis_index("expert")
    x, c = p // NC, p % NC
    y, z = e // NZ, e % NZ
    half = z // 4

    def at(xx, cc, yy, zz):
        return (xx * NC + cc, yy * NZ + zz)

    def z_dev(zz):
        return at(x, c, y, zz)

    def y_dev(yy):
        return at(x, c, yy, z)

    def x_dev(xx):
        return at(xx, c, y, z)

    core_dev = at(x, 1 - c, y, z)

    def remote(src, dst, ss, rs, dev):
        return pltpu.make_async_remote_copy(
            src_ref=src, dst_ref=dst, send_sem=ss, recv_sem=rs, device_id=dev, device_id_type=MESH
        )

    loads = [
        pltpu.make_async_copy(src.at[0], dst, load_sem.at[i])
        for i, (src, dst) in enumerate(
            ((wd_hbm, wd), (gpre_hbm, gpre), (upre_hbm, upre), (wg_hbm, wg), (wu_hbm, wu))
        )
    ]
    for load in loads:
        load.start()

    upg[z] = upper_ref[...]
    kept = slot_ref[...] >= 0
    metag[z] = jnp.zeros((TOK, 128), F32)
    metag[z, :, 0:4] = jnp.where(kept, ids_ref[...] * CAP + slot_ref[...], -1).astype(F32)
    metag[z, :, 4:8] = prob_ref[...]
    kvg[e, :, 0:128] = k_ref[...]
    kvg[e, :, 128:256] = v_ref[...]

    barrier = pltpu.get_barrier_semaphore()
    peers = (
        [z_dev((z + k) % NZ) for k in range(1, NZ)]
        + [y_dev((y + k) % NY) for k in range(1, NY)]
        + [x_dev((x + k) % NX) for k in range(1, NX)]
        + [core_dev]
    )
    for peer in peers:
        pl.semaphore_signal(barrier, inc=1, device_id=peer, device_id_type=MESH)
    pl.semaphore_wait(barrier, len(peers))

    z_order = (1, 7, 2, 6, 3, 5, 4)
    y_order = (1, 3, 2)

    def up_copy(zsrc, zdst):
        return remote(upg.at[zsrc], upg.at[zsrc], up_s.at[zdst], up_r.at[zsrc], z_dev(zdst))

    def meta_copy(zsrc, zdst):
        return remote(metag.at[zsrc], metag.at[zsrc], meta_s.at[zdst], meta_r.at[zsrc], z_dev(zdst))

    def kvz_copy(zsrc, zdst):
        blk = kvg.at[y * NZ + zsrc]
        return remote(blk, blk, kvz_s.at[zdst], kvz_r.at[zsrc], z_dev(zdst))

    for k in z_order:
        up_copy(z, (z + k) % NZ).start()
        meta_copy(z, (z + k) % NZ).start()
    for k in z_order:
        kvz_copy(z, (z + k) % NZ).start()

    for g in range(GROUP):
        cols = slice(g * 128, (g + 1) * 128)
        qrows[g * 128:(g + 1) * 128, :] = q_ref[:, cols]
        dorows[g * 128:(g + 1) * 128, :] = do_ref[:, cols]
        prod = do_ref[:, cols].astype(F32) * o_ref[:, cols].astype(F32)
        delta[:, cols] = jnp.sum(prod.T, axis=0, keepdims=True)

    col = lax.broadcasted_iota(jnp.int32, (TOK, 4 * PAIR_SLOTS), 1)
    col_y = (
        (col >= PAIR_SLOTS).astype(jnp.int32)
        + (col >= 2 * PAIR_SLOTS).astype(jnp.int32)
        + (col >= 3 * PAIR_SLOTS).astype(jnp.int32)
    )
    col_in = col - PAIR_SLOTS * col_y
    col_i = (col_in >= CAP).astype(jnp.int32)
    wanted = (2 * col_y + half) * CAP + (col_in - CAP * col_i)

    def slot_copy(yrel, pair):
        ydst = (y + yrel) % NY
        rows = pl.ds(pl.multiple_of(pair * PAIR_SLOTS, 16), PAIR_SLOTS)
        return remote(
            sbuf.at[ydst, rows], arrived.at[y, rows], sl_s.at[yrel - 1, pair], sl_r.at[yrel - 1, pair], y_dev(ydst)
        )

    for j in (0, 1, 3, 2):
        pair = (z // 2 + j) % PAIRS
        for i in range(2):
            zz = pair * 2 + i

            @pl.when(zz != z)
            def _():
                up_copy(zz, z).wait_recv()
                meta_copy(zz, z).wait_recv()

            meta = metag[zz]
            tokens = upg[zz].astype(F32)
            target = meta[:, 0:4].astype(jnp.int32)
            mine = jnp.where(col_i == i, wanted, -2)
            table = jnp.zeros((TOK, 4 * PAIR_SLOTS), F32)
            for k in range(4):
                row = (i * 4 + k) * TOK
                stack[row:row + TOK, :] = (meta[:, 4 + k:5 + k] * tokens).astype(BF16)
                hit = (target[:, k:k + 1] == mine).astype(F32)
                table = table + hit
                picks[row:row + TOK, :] = hit.astype(BF16)
            tables[pair, i * TOK:(i + 1) * TOK, :] = table.astype(BF16)
        picked = dot(picks[...], stack[...], TN).astype(BF16)
        rows = pl.ds(pl.multiple_of(pair * PAIR_SLOTS, 16), PAIR_SLOTS)
        for yy in range(NY):
            sbuf[yy, rows, :] = picked[yy * PAIR_SLOTS:(yy + 1) * PAIR_SLOTS]
        arrived[y, rows, :] = sbuf[y, rows, :]
        for yrel in y_order:
            slot_copy(yrel, pair).start()

    def kvy_copy(ysrc, yrel, zz):
        blk = kvg.at[ysrc * NZ + zz]
        return remote(blk, blk, kvy_s.at[yrel - 1, zz], kvy_r.at[yrel - 1, zz], y_dev((ysrc + yrel) % NY))

    def kv_forward(k, carry):
        zz = (z + k) % NZ

        @pl.when(k > 0)
        def _():
            kvz_copy(zz, z).wait_recv()

        for yrel in range(1, NY):

            @pl.when(y + yrel < NY)
            def _():
                kvy_copy(y, yrel, zz).start()

        return carry

    lax.fori_loop(0, NZ, kv_forward, 0)

    loads[0].wait()

    def core_copy(xx):
        return remote(csend.at[xx], crecv.at[xx], core_s.at[xx], core_r.at[xx], core_dev)

    for yrel in (0, 1, 3, 2):
        ysrc = (y - yrel + NY) % NY
        if yrel > 0:
            for pair in range(PAIRS):
                rows = pl.ds(pair * PAIR_SLOTS, PAIR_SLOTS)
                remote(
                    sbuf.at[ysrc, rows], arrived.at[ysrc, rows], sl_s.at[yrel - 1, pair], sl_r.at[yrel - 1, pair], y_dev(ysrc)
                ).wait_recv()
        part = dot(arrived[ysrc], wd[...], NT)
        hpart[ysrc, 0] = part[0:HALF_SLOTS]
        hpart[ysrc, 1] = part[HALF_SLOTS:]
        csend[ysrc] = hpart[ysrc, 1 - c].astype(BF16)
        core_copy(ysrc).start()

    def xr_copy(xrel):
        xdst = (x + xrel) % NX
        return remote(xsend.at[xdst], xrecv.at[xrel - 1], xr_s.at[xrel - 1], xr_r.at[xrel - 1], x_dev(xdst))

    for xrel in (2, 1, 3, 0):
        xx = (x + xrel) % NX
        core_copy(xx).wait_recv()
        total = hpart[xx, c] + crecv[xx].astype(F32)
        if xrel > 0:
            xsend[xx] = total.astype(BF16)
            xr_copy(xrel).start()
        else:
            hpart[xx, c] = total

    def score_block(b, masked):
        keys = kvg[pl.ds(2 * b, 2), :, 0:128].reshape(KEYS, 128)
        s = dot(keys, qrows[...], NT) * SCALE
        if masked:
            key_pos = b * KEYS + lax.broadcasted_iota(jnp.int32, (KEYS, ROWS), 0)
            row_pos = e * ATT + (lax.broadcasted_iota(jnp.int32, (KEYS, ROWS), 1) & 127)
            s = jnp.where(key_pos <= row_pos, s, MASKED)
        scores[b] = s
        mrun[...] = jnp.maximum(mrun[...], jnp.max(s.reshape(KEYS // 8, 8, ROWS), axis=0))

    def score_step(b, carry):
        score_block(b, False)
        return carry

    last = e // 2
    mrun[...] = jnp.full((8, ROWS), MASKED, F32)
    score_block(last, True)
    lax.fori_loop(y * PAIRS, last, score_step, 0)

    hsum = hpart[x, c]
    for xrel in (1, 3, 2):
        xr_copy(xrel).wait_recv()
        hsum = hsum + xrecv[xrel - 1].astype(F32)
    hidg[x, c] = hsum.astype(BF16)

    def xg_copy(xsrc, xrel):
        blk = hidg.at[xsrc, c]
        return remote(blk, blk, xg_s.at[xrel - 1], xg_r.at[xrel - 1], x_dev((xsrc + xrel) % NX))

    def cg_copy(xx, cc):
        blk = hidg.at[xx, cc]
        return remote(blk, blk, cg_s.at[xx], cg_r.at[xx], core_dev)

    for xrel in (2, 1, 3):
        xg_copy(x, xrel).start()
    cg_copy(x, c).start()

    for yrel in range(1, NY):

        @pl.when(y >= yrel)
        def _():
            ysrc = y - yrel

            def kv_wait(zz, carry):
                kvy_copy(ysrc, yrel, zz).wait_recv()
                return carry

            lax.fori_loop(0, NZ, kv_wait, 0)
            lax.fori_loop(ysrc * PAIRS, ysrc * PAIRS + PAIRS, score_step, 0)

    top = jnp.max(mrun[...], axis=0, keepdims=True)
    lrun[...] = jnp.zeros((8, ROWS), F32)

    def sum_step(b, carry):
        lrun[...] += jnp.sum(jnp.exp(scores[b] - top).reshape(KEYS // 8, 8, ROWS), axis=0)
        return carry

    lax.fori_loop(0, last + 1, sum_step, 0)
    log_total = top + jnp.log(jnp.sum(lrun[...], axis=0, keepdims=True))

    for load in loads[1:]:
        load.wait()

    def t_copy(yrel):
        ydst = (y + yrel) % NY
        return remote(tsend.at[ydst], trecv.at[:, y], t_s.at[yrel - 1], t_r.at[yrel - 1], y_dev(ydst))

    for xrel in (0, 1, 3, 2):
        xx = (x - xrel + NX) % NX
        if xrel > 0:
            xg_copy(xx, xrel).wait_recv()
            cg_copy(xx, c).start()
        cg_copy(xx, 1 - c).wait_recv()
        rows = pl.ds(pl.multiple_of(xx * ROW_SLOTS, 16), ROW_SLOTS)
        hid = hidg[xx].reshape(ROW_SLOTS, UNITS).astype(F32)
        a = gpre[rows, :].astype(F32)
        b = upre[rows, :].astype(F32)
        s = 1.0 / (1.0 + jnp.exp(-a))
        hs = hid * s
        gate_grad = (hs * b * (1.0 + a * (1.0 - s))).astype(BF16)
        up_grad = (hs * a).astype(BF16)
        terms = dot(gate_grad, wg[...], NT) + dot(up_grad, wu[...], NT)
        tsend[xx] = terms.astype(BF16).reshape(PAIRS, PAIR_SLOTS, COLS)

        @pl.when(xx == y)
        def _():
            trecv[:, y] = tsend[xx]

        for yrel in range(1, NY):

            @pl.when((y + yrel) % NY == xx)
            def _():
                t_copy(yrel).start()

    dqt[...] = jnp.zeros((128, ROWS), F32)
    row_delta = delta[...]

    def grad_block(b):
        keys = kvg[pl.ds(2 * b, 2), :, 0:128].reshape(KEYS, 128)
        values = kvg[pl.ds(2 * b, 2), :, 128:256].reshape(KEYS, 128)
        probs = jnp.exp(scores[b] - log_total)
        grad_probs = dot(values, dorows[...], NT)
        ds = (probs * (grad_probs - row_delta) * SCALE).astype(BF16)
        dqt[...] += dot(keys, ds, TN)
        dkv[pl.ds(2 * b, 2), :, 0:128] = dot(ds, qrows[...], NN).astype(BF16).reshape(2, ATT, 128)
        dkv[pl.ds(2 * b, 2), :, 128:256] = dot(probs.astype(BF16), dorows[...], NN).astype(BF16).reshape(2, ATT, 128)

    def dy_copy(yrel, ydst, blk):
        src = dkv.at[pl.ds(ydst * NZ + 2 * blk, 2)]
        return remote(src, drecv.at[yrel - 1, pl.ds(2 * blk, 2)], dy_s.at[yrel - 1, blk], dy_r.at[yrel - 1, blk], y_dev(ydst))

    for yrel in range(1, NY):

        @pl.when(y >= yrel)
        def _():
            def row_step(blk, carry):
                grad_block((y - yrel) * PAIRS + blk)
                dy_copy(yrel, y - yrel, blk).start()
                return carry

            lax.fori_loop(0, PAIRS, row_step, 0)

    def own_step(blk, carry):
        b = y * PAIRS + blk

        @pl.when(b <= last)
        def _():
            grad_block(b)

        @pl.when(b > last)
        def _():
            dkv[pl.ds(2 * b, 2)] = jnp.zeros((2, ATT, 256), BF16)

        return carry

    lax.fori_loop(0, PAIRS, own_step, 0)
    for g in range(GROUP):
        cols = slice(g * 128, (g + 1) * 128)
        dq_ref[:, cols] = dqt[:, cols].T.astype(BF16)

    for yrel in y_order:
        ysrc = (y - yrel + NY) % NY
        remote(
            tsend.at[y], trecv.at[:, ysrc], t_s.at[yrel - 1], t_r.at[yrel - 1], y_dev(ysrc)
        ).wait_recv()

    def tz_copy(zsrc, zdst):
        return remote(zsend.at[zdst], zrecv.at[zsrc], tz_s.at[zdst], tz_r.at[zsrc], z_dev(zdst))

    for j in (2, 1, 3, 0):
        pair = (z // 2 + j) % PAIRS
        tokens = dot(tables[pair], trecv[pair].reshape(ROW_SLOTS, COLS), NN)
        for i in range(2):
            zz = pair * 2 + i
            part = tokens[i * TOK:(i + 1) * TOK]

            @pl.when(zz == z)
            def _():
                mown[...] = part

            @pl.when(zz != z)
            def _():
                zsend[zz] = part.astype(BF16)
                tz_copy(z, zz).start()

    def dz_copy(zsrc, zdst):
        return remote(dzsend.at[zdst], dzrecv.at[zsrc], dz_s.at[zdst], dz_r.at[zsrc], z_dev(zdst))

    for yrel in range(1, NY):

        @pl.when(y + yrel < NY)
        def _():
            def dy_wait(blk, carry):
                dst = drecv.at[yrel - 1, pl.ds(2 * blk, 2)]
                remote(dst, dst, dy_s.at[yrel - 1, blk], dy_r.at[yrel - 1, blk], y_dev((y + yrel) % NY)).wait_recv()
                return carry

            lax.fori_loop(0, PAIRS, dy_wait, 0)

    def dz_step(k, carry):
        zz = (z + k) % NZ
        dtmp[...] = dkv[y * NZ + zz].astype(F32)
        for yrel in range(1, NY):

            @pl.when(y + yrel < NY)
            def _():
                dtmp[...] += drecv[yrel - 1, zz].astype(F32)

        @pl.when(k < NZ)
        def _():
            dzsend[zz] = dtmp[...].astype(BF16)
            dz_copy(z, zz).start()

        return carry

    lax.fori_loop(1, NZ + 1, dz_step, 0)

    acc = mown[...] + upper_ref[...].astype(F32)
    for k in z_order:
        zz = (z + k) % NZ
        tz_copy(zz, z).wait_recv()
        acc = acc + zrecv[zz].astype(F32)
    moe_ref[...] = acc.astype(BF16)

    for k in z_order:
        zz = (z + k) % NZ
        dz_copy(zz, z).wait_recv()
        dtmp[...] += dzrecv[zz].astype(F32)
    dk_ref[...] = dtmp[:, 0:128].astype(BF16)
    dv_ref[...] = dtmp[:, 128:256].astype(BF16)

    for k in z_order:
        zz = (z + k) % NZ
        up_copy(z, zz).wait_send()
        meta_copy(z, zz).wait_send()
        kvz_copy(z, zz).wait_send()
        tz_copy(z, zz).wait_send()
        dz_copy(z, zz).wait_send()
    for yrel in range(1, NY):
        for pair in range(PAIRS):
            slot_copy(yrel, pair).wait_send()
        t_copy(yrel).wait_send()

        @pl.when(y + yrel < NY)
        def _():
            def kvy_sent(zz, carry):
                kvy_copy(y, yrel, zz).wait_send()
                return carry

            lax.fori_loop(0, NZ, kvy_sent, 0)

        @pl.when(y >= yrel)
        def _():
            def dy_sent(blk, carry):
                dy_copy(yrel, y - yrel, blk).wait_send()
                return carry

            lax.fori_loop(0, PAIRS, dy_sent, 0)

    for xrel in range(1, NX):
        xr_copy(xrel).wait_send()
        xg_copy(x, xrel).wait_send()
    for xx in range(NX):
        core_copy(xx).wait_send()
        cg_copy(xx, c).wait_send()


def vmem(*shape, dtype=BF16):
    return pltpu.VMEM(shape, dtype)


def on_device(*args):
    dma = pltpu.SemaphoreType.DMA
    whole = pl.BlockSpec(memory_space=pltpu.VMEM)
    anywhere = pl.BlockSpec(memory_space=pl.ANY)
    outs = [(TOK, COLS), (ATT, COLS), (ATT, HEAD_DIM), (ATT, HEAD_DIM)]
    return pl.pallas_call(
        kernel,
        out_shape=[jax.ShapeDtypeStruct(shape, BF16) for shape in outs],
        in_specs=[whole] * 4 + [anywhere] * 5 + [whole] * 5,
        out_specs=[whole] * 4,
        scratch_shapes=[
            vmem(COLS, UNITS), vmem(COLS, UNITS), vmem(COLS, UNITS), vmem(COLS, UNITS), vmem(UNITS, COLS), dma((5,)),
            vmem(NZ, TOK, COLS), vmem(NZ, TOK, 128, dtype=F32), vmem(8 * TOK, COLS), vmem(8 * TOK, ROW_SLOTS),
            vmem(PAIRS, 2 * TOK, ROW_SLOTS), vmem(NY, ROW_SLOTS, COLS), vmem(NY, ROW_SLOTS, COLS),
            vmem(NX, NC, HALF_SLOTS, UNITS, dtype=F32), vmem(NX, HALF_SLOTS, UNITS), vmem(NX, HALF_SLOTS, UNITS),
            vmem(NX, HALF_SLOTS, UNITS), vmem(NX - 1, HALF_SLOTS, UNITS), vmem(NX, NC, HALF_SLOTS, UNITS),
            vmem(NY, PAIRS, PAIR_SLOTS, COLS), vmem(PAIRS, NY, PAIR_SLOTS, COLS),
            vmem(NZ, TOK, COLS), vmem(NZ, TOK, COLS), vmem(TOK, COLS, dtype=F32),
            vmem(NY * NZ, ATT, 256), vmem(ROWS, 128), vmem(ROWS, 128), vmem(1, ROWS, dtype=F32),
            vmem(BLOCKS, KEYS, ROWS, dtype=F32), vmem(8, ROWS, dtype=F32), vmem(8, ROWS, dtype=F32),
            vmem(128, ROWS, dtype=F32), vmem(NY * NZ, ATT, 256), vmem(NY - 1, NZ, ATT, 256),
            vmem(NZ, ATT, 256), vmem(NZ, ATT, 256), vmem(ATT, 256, dtype=F32),
            dma((NZ,)), dma((NZ,)), dma((NZ,)), dma((NZ,)), dma((NZ,)), dma((NZ,)),
            dma((NY - 1, NZ)), dma((NY - 1, NZ)), dma((NY - 1, PAIRS)), dma((NY - 1, PAIRS)),
            dma((NX,)), dma((NX,)), dma((NX - 1,)), dma((NX - 1,)), dma((NX - 1,)), dma((NX - 1,)), dma((NX,)), dma((NX,)),
            dma((NY - 1,)), dma((NY - 1,)), dma((NZ,)), dma((NZ,)),
            dma((NY - 1, PAIRS)), dma((NY - 1, PAIRS)), dma((NZ,)), dma((NZ,)),
        ],
        compiler_params=pltpu.CompilerParams(
            collective_id=0, has_side_effects=True, vmem_limit_bytes=60 * 1024 * 1024
        ),
        cost_estimate=pl.CostEstimate(flops=9_000_000_000, bytes_accessed=14_000_000, transcendentals=8_000_000),
        name="layer_grad",
    )(*args)


def solution(mesh):
    return jax.shard_map(
        on_device,
        mesh=mesh,
        in_specs=(
            P("expert", "pipe"),
            P("expert", None),
            P("expert", None),
            P("expert", None),
            P("expert", None, None),
            P("expert", None, None),
            P("expert", "pipe", None),
            P("expert", "pipe", None),
            P("expert", None, "pipe"),
            P("expert", "pipe"),
            P("expert", "pipe"),
            P("expert", "pipe"),
            P("expert", "pipe"),
            P("expert", "pipe"),
        ),
        out_specs=(
            P("expert", "pipe"),
            P("expert", "pipe"),
            P("expert", "pipe"),
            P("expert", "pipe"),
        ),
        check_vma=False,
    )
```

```python
import jax
import jax.numpy as jnp
from jax import lax
from jax.experimental import pallas as pl
from jax.experimental.pallas import tpu as pltpu
from jax.sharding import PartitionSpec as P

MESH = pl.DeviceIdType.MESH
F32 = jnp.float32
BF16 = jnp.bfloat16

EXPERTS = 8
HEAD_DIM = 128
GROUP = 6
TOK = 32
ATT = 128
CAP = 24
UNITS = 1344
COLS = 768
HALF_COLS = COLS // 2
ROWS = GROUP * ATT
NX, NC, NY, NZ = 4, 2, 4, 8
PAIRS = NZ // 2
PAIR_SLOTS = 2 * CAP
ROW_SLOTS = NZ * CAP
KEYS = 2 * ATT
BLOCKS = NY * PAIRS
SCALE = HEAD_DIM ** (-0.5)
MASKED = -1e30

NT = (((1,), (1,)), ((), ()))
TN = (((0,), (0,)), ((), ()))
NN = (((1,), (0,)), ((), ()))


def dot(a, b, dims):
    return lax.dot_general(a, b, dims, preferred_element_type=F32)


def kernel(
    upper_ref, ids_ref, slot_ref, prob_ref, gpre_hbm, upre_hbm, wg_hbm, wu_hbm, wd_hbm,
    q_hbm, k_hbm, v_hbm, o_hbm, do_hbm,
    moe_ref, dq_ref, dk_ref, dv_ref,
    gpre, upre, gpre_t, upre_t, wg, wu, wd, q_ref, o_ref, do_ref, load_sem,
    upg, metag, stack, picks, tables, sbuf, arrived,
    hpart, csend, crecv, xsend, xrecv, hown, hidg,
    tsend, trecv, zsend, zrecv, mown,
    kg, vg, qrows, dorows, delta, scores, mrun, lrun, stat, dqt, dkv, drecv, d2recv, d2sum, d2in, dzsend, dzrecv, dtmp, down,
    up_s, up_r, meta_s, meta_r, kvz_s, kvz_r, kvy_s, kvy_r, sl_s, sl_r,
    core_s, core_r, xr_s, xr_r, xg_s, xg_r, cg_s, cg_r, t_s, t_r, tz_s, tz_r,
    dy_s, dy_r, dz_s, dz_r, kv2y_s, kv2y_r, kv2z_s, kv2z_r, d2z_s, d2z_r, d2y_s, d2y_r,
):
    p = lax.axis_index("pipe")
    e = lax.axis_index("expert")
    x, c = p // NC, p % NC
    y, z = e // NZ, e % NZ
    half = z // 4

    def at(xx, cc, yy, zz):
        return (xx * NC + cc, yy * NZ + zz)

    def z_dev(zz):
        return at(x, c, y, zz)

    def y_dev(yy):
        return at(x, c, yy, z)

    def x_dev(xx):
        return at(xx, c, y, z)

    core_dev = at(x, 1 - c, y, z)

    def remote(src, dst, ss, rs, dev):
        return pltpu.make_async_remote_copy(
            src_ref=src, dst_ref=dst, send_sem=ss, recv_sem=rs, device_id=dev, device_id_type=MESH
        )

    loads = [
        pltpu.make_async_copy(src, dst, load_sem.at[i])
        for i, (src, dst) in enumerate(
            (
                (wd_hbm.at[0], wd), (gpre_hbm.at[0], gpre_t), (upre_hbm.at[0], upre_t), (wg_hbm.at[0], wg), (wu_hbm.at[0], wu),
                (k_hbm, kg.at[e]), (v_hbm, vg.at[e]), (q_hbm, q_ref), (o_hbm, o_ref), (do_hbm, do_ref),
            )
        )
    ]
    for n in (5, 6, 1, 2, 0, 7, 9, 8, 3, 4):
        loads[n].start()

    upg[z] = upper_ref[...]
    kept = slot_ref[...] >= 0
    dtmp[...] = jnp.zeros((ATT, 256), F32)
    dtmp[0:4, 0:TOK] = jnp.where(kept, ids_ref[...] * CAP + slot_ref[...], -1).astype(F32)
    dtmp[4:8, 0:TOK] = prob_ref[...]
    metag[z] = dtmp[:, 0:128].T[0:TOK]

    barrier = pltpu.get_barrier_semaphore()
    peers = (
        [z_dev((z + k) % NZ) for k in range(1, NZ)]
        + [y_dev((y + k) % NY) for k in range(1, NY)]
        + [x_dev((x + k) % NX) for k in range(1, NX)]
        + [core_dev]
    )
    for peer in peers:
        pl.semaphore_signal(barrier, inc=1, device_id=peer, device_id_type=MESH)
    pl.semaphore_wait(barrier, len(peers))

    z_order = (1, 7, 2, 6, 3, 5, 4)
    y_order = (1, 3, 2)

    def up_copy(zsrc, zdst):
        return remote(upg.at[zsrc], upg.at[zsrc], up_s.at[zdst], up_r.at[zsrc], z_dev(zdst))

    def meta_copy(zsrc, zdst):
        return remote(metag.at[zsrc], metag.at[zsrc], meta_s.at[zdst], meta_r.at[zsrc], z_dev(zdst))

    def kvz_needed(zsrc, zdst):
        return (y < NY - 1) | (zdst // 2 >= zsrc // 2)

    def kv2y_copy(buf, n, ysrc):
        blk = buf.at[ysrc * NZ + z]
        return remote(blk, blk, kv2y_s.at[n], kv2y_r.at[n], y_dev((ysrc + 2) % NY))

    def kv2z_copy(buf, n, zsrc, zdst):
        blk = buf.at[(y - 2) * NZ + zsrc]
        return remote(blk, blk, kv2z_s.at[n, zdst], kv2z_r.at[n, zsrc], z_dev(zdst))

    def kvz_copy(buf, n, zsrc, zdst):
        blk = buf.at[y * NZ + zsrc]
        return remote(blk, blk, kvz_s.at[n, zdst], kvz_r.at[n, zsrc], z_dev(zdst))

    for k in z_order:
        up_copy(z, (z + k) % NZ).start()
        meta_copy(z, (z + k) % NZ).start()
    col = lax.broadcasted_iota(jnp.int32, (TOK, 4 * PAIR_SLOTS), 1)
    col_y = (
        (col >= PAIR_SLOTS).astype(jnp.int32)
        + (col >= 2 * PAIR_SLOTS).astype(jnp.int32)
        + (col >= 3 * PAIR_SLOTS).astype(jnp.int32)
    )
    col_in = col - PAIR_SLOTS * col_y
    col_i = (col_in >= CAP).astype(jnp.int32)
    wanted = (2 * col_y + half) * CAP + (col_in - CAP * col_i)

    def slot_copy(yrel, pair):
        ydst = (y + yrel) % NY
        rows = pl.ds(pl.multiple_of(pair * PAIR_SLOTS, 16), PAIR_SLOTS)
        return remote(
            sbuf.at[ydst, rows], arrived.at[y, rows], sl_s.at[yrel - 1, pair], sl_r.at[yrel - 1, pair], y_dev(ydst)
        )

    sources = ((1, 2), (3, 0))

    def source_row(h, cc):
        return (y + NY - jnp.where(cc == 0, sources[h][0], sources[h][1])) % NY

    def core_copy(h):
        return remote(csend.at[h], crecv.at[h], core_s.at[h], core_r.at[h], core_dev)

    def xr_copy(h, xrel):
        xdst = (x + xrel) % NX
        return remote(
            xsend.at[h, xdst], xrecv.at[h, xrel - 1], xr_s.at[h, xrel - 1], xr_r.at[h, xrel - 1], x_dev(xdst)
        )

    def slots_wait(yrel):
        ysrc = (y - yrel + NY) % NY
        for pair in range(PAIRS):
            rows = pl.ds(pair * PAIR_SLOTS, PAIR_SLOTS)
            remote(
                sbuf.at[ysrc, rows], arrived.at[ysrc, rows], sl_s.at[yrel - 1, pair], sl_r.at[yrel - 1, pair], y_dev(ysrc)
            ).wait_recv()

    def hidden_other(h):
        csend[h] = dot(arrived[source_row(h, 1 - c)], wd[...], NT).astype(BF16)
        core_copy(h).start()

    def hidden_mine(h):
        hpart[h] = dot(arrived[source_row(h, c)], wd[...], NT)

    def hidden_sum(h):
        core_copy(h).wait_recv()
        for xrel in (2, 1, 3, 0):
            xx = (x + xrel) % NX
            rows = pl.ds(pl.multiple_of(xx * PAIR_SLOTS, 16), PAIR_SLOTS)
            total = hpart[h, rows] + crecv[h, rows].astype(F32)
            if xrel > 0:
                xsend[h, xx] = total.astype(BF16)
                xr_copy(h, xrel).start()
            else:
                hown[h] = total

    def kvy_copy(buf, n, ysrc, yrel, zz):
        blk = buf.at[ysrc * NZ + zz]
        return remote(blk, blk, kvy_s.at[n, yrel - 1, zz], kvy_r.at[n, yrel - 1, zz], y_dev((ysrc + yrel) % NY))

    def kv_on(n):
        buf = (kg, vg)[n]

        def kv_forward(k, carry):
            zz = (z + k) % NZ

            @pl.when((k > 0) & kvz_needed(zz, z))
            def _():
                kvz_copy(buf, n, zz, z).wait_recv()

            for yrel in (1, 3):

                @pl.when(y + yrel < NY)
                def _():
                    kvy_copy(buf, n, y, yrel, zz).start()

            return carry

        lax.fori_loop(0, NZ, kv_forward, 0)

    def score_block(b, masked):
        keys = kg[pl.ds(2 * b, 2)].reshape(KEYS, 128)
        s = dot(keys, qrows[...], NT) * SCALE
        if masked:
            key_pos = b * KEYS + lax.broadcasted_iota(jnp.int32, (KEYS, ROWS), 0)
            row_pos = e * ATT + (lax.broadcasted_iota(jnp.int32, (KEYS, ROWS), 1) & 127)
            s = jnp.where(key_pos <= row_pos, s, MASKED)
        scores[b] = s
        mrun[...] = jnp.maximum(mrun[...], jnp.max(s.reshape(KEYS // 8, 8, ROWS), axis=0))

    def score_step(b, carry):
        score_block(b, False)
        return carry

    last = e // 2

    def xg_copy(h, xsrc, xrel):
        blk = hidg.at[h, c, xsrc]
        return remote(blk, blk, xg_s.at[h, xrel - 1], xg_r.at[h, xrel - 1], x_dev((xsrc + xrel) % NX))

    def cg_copy(h, xx, cc):
        blk = hidg.at[h, cc, xx]
        return remote(blk, blk, cg_s.at[h, xx], cg_r.at[h, xx], core_dev)

    def t_copy(n, yrel):
        ydst = (y + yrel) % NY
        return remote(tsend.at[ydst, n], trecv.at[n, :, y], t_s.at[n, yrel - 1], t_r.at[n, yrel - 1], y_dev(ydst))

    def slot_terms(h, cc):
        ysrc = source_row(h, cc)
        rows = pl.ds(pl.multiple_of(ysrc * ROW_SLOTS, 16), ROW_SLOTS)
        hid = hidg[h, cc].reshape(ROW_SLOTS, UNITS).astype(F32)
        a = gpre[rows, :].astype(F32)
        b = upre[rows, :].astype(F32)
        s = 1.0 / (1.0 + jnp.exp(-a))
        hs = hid * s
        gate_grad = (hs * b * (1.0 + a * (1.0 - s))).astype(BF16)
        up_grad = (hs * a).astype(BF16)
        rel = (ysrc - y + NY) % NY
        for n in range(2):
            cols = slice(n * HALF_COLS, (n + 1) * HALF_COLS)
            part = dot(gate_grad, wg[:, cols], NN) + dot(up_grad, wu[:, cols], NN)
            tsend[ysrc, n] = part.astype(BF16).reshape(PAIRS, PAIR_SLOTS, HALF_COLS)

            @pl.when(rel == 0)
            def _():
                trecv[n, :, y] = tsend[y, n]

            @pl.when(rel > 0)
            def _():
                t_copy(n, rel).start()

    def grad_block(b):
        keys = kg[pl.ds(2 * b, 2)].reshape(KEYS, 128)
        values = vg[pl.ds(2 * b, 2)].reshape(KEYS, 128)
        probs = jnp.exp(scores[b] - stat[...])
        grad_probs = dot(values, dorows[...], NT)
        ds = (probs * (grad_probs - delta[...]) * SCALE).astype(BF16)
        dqt[...] += dot(keys, ds, TN)
        dkv[pl.ds(2 * b, 2), :, 0:128] = dot(ds, qrows[...], NN).astype(BF16).reshape(2, ATT, 128)
        dkv[pl.ds(2 * b, 2), :, 128:256] = dot(probs.astype(BF16), dorows[...], NN).astype(BF16).reshape(2, ATT, 128)

    def dy_copy(yrel, ydst, blk):
        src = dkv.at[pl.ds(ydst * NZ + 2 * blk, 2)]
        return remote(src, drecv.at[yrel - 1, pl.ds(2 * blk, 2)], dy_s.at[yrel - 1, blk], dy_r.at[yrel - 1, blk], y_dev(ydst))

    def d2z_copy(zsrc, zdst):
        return remote(
            dkv.at[(y - 2) * NZ + zdst], d2recv.at[zsrc], d2z_s.at[zdst], d2z_r.at[zsrc], z_dev(zdst)
        )

    def d2y_copy(ydst):
        return remote(d2sum, d2in, d2y_s.at[0], d2y_r.at[0], y_dev(ydst))

    def row_sum():
        @pl.when(y >= 2)
        def _():
            dtmp[...] = dkv[(y - 2) * NZ + z].astype(F32)
            for k in z_order:
                zz = (z + k) % NZ
                d2z_copy(zz, z).wait_recv()
                dtmp[...] += d2recv[zz].astype(F32)
            d2sum[...] = dtmp[...].astype(BF16)
            d2y_copy((y + 2) % NY).start()

    def tz_copy(n, zsrc, zdst):
        return remote(zsend.at[n, zdst], zrecv.at[n, zsrc], tz_s.at[n, zdst], tz_r.at[n, zsrc], z_dev(zdst))

    def send_kv():
        for n, buf in enumerate((kg, vg)):

            @pl.when(y < 2)
            def _():
                kv2y_copy(buf, n, y).start()

        for n, buf in enumerate((kg, vg)):
            for k in z_order:
                zdst = (z + k) % NZ

                @pl.when(kvz_needed(z, zdst))
                def _():
                    kvz_copy(buf, n, z, zdst).start()

    def kv2_on(n):
        buf = (kg, vg)[n]

        @pl.when(y >= 2)
        def _():
            kv2y_copy(buf, n, y - 2).wait_recv()
            for k in z_order:
                kv2z_copy(buf, n, z, (z + k) % NZ).start()

    def kv2_wait(n):
        for k in z_order:
            kv2z_copy((kg, vg)[n], n, (z + k) % NZ, z).wait_recv()

    def turn_gate():
        loads[1].wait()
        for i in range(COLS // 128):
            cols = slice(i * 128, (i + 1) * 128)
            gpre[cols, :] = gpre_t[:, cols].T

    def turn_up():
        loads[2].wait()
        for i in range(COLS // 128):
            cols = slice(i * 128, (i + 1) * 128)
            upre[cols, :] = upre_t[:, cols].T

    def prepare():
        for n in (7, 8, 9):
            loads[n].wait()
        for g in range(GROUP):
            cols = slice(g * 128, (g + 1) * 128)
            qrows[g * 128:(g + 1) * 128, :] = q_ref[:, cols]
            dorows[g * 128:(g + 1) * 128, :] = do_ref[:, cols]
            prod = do_ref[:, cols].astype(F32) * o_ref[:, cols].astype(F32)
            delta[:, cols] = jnp.sum(prod.T, axis=0, keepdims=True)

    def dispatch():
        for j in (0, 1, 3, 2):
            pair = (z // 2 + j) % PAIRS
            for i in range(2):
                zz = pair * 2 + i

                @pl.when(zz != z)
                def _():
                    up_copy(zz, z).wait_recv()
                    meta_copy(zz, z).wait_recv()

                meta = metag[zz]
                tokens = upg[zz].astype(F32)
                target = meta[:, 0:4].astype(jnp.int32)
                mine = jnp.where(col_i == i, wanted, -2)
                table = jnp.zeros((TOK, 4 * PAIR_SLOTS), F32)
                for k in range(4):
                    row = (i * 4 + k) * TOK
                    stack[row:row + TOK, :] = (meta[:, 4 + k:5 + k] * tokens).astype(BF16)
                    hit = (target[:, k:k + 1] == mine).astype(F32)
                    table = table + hit
                    picks[row:row + TOK, :] = hit.astype(BF16)
                tables[pair, i * TOK:(i + 1) * TOK, :] = table.astype(BF16)
            picked = dot(picks[...], stack[...], TN).astype(BF16)
            rows = pl.ds(pl.multiple_of(pair * PAIR_SLOTS, 16), PAIR_SLOTS)
            for yy in range(NY):
                sbuf[yy, rows, :] = picked[yy * PAIR_SLOTS:(yy + 1) * PAIR_SLOTS]
            arrived[y, rows, :] = sbuf[y, rows, :]
            for yrel in y_order:
                slot_copy(yrel, pair).start()

    def own_scores():
        mrun[...] = jnp.full((8, ROWS), MASKED, F32)
        score_block(last, True)
        lax.fori_loop(y * PAIRS, last, score_step, 0)

    def row_scores(yrel):
        @pl.when(y >= yrel)
        def _():
            ysrc = y - yrel

            def k_wait(zz, carry):
                kvy_copy(kg, 0, ysrc, yrel, zz).wait_recv()
                return carry

            if yrel == 2:
                kv2_wait(0)
            else:
                lax.fori_loop(0, NZ, k_wait, 0)
            lax.fori_loop(ysrc * PAIRS, ysrc * PAIRS + PAIRS, score_step, 0)

    def totals():
        top = jnp.max(mrun[...], axis=0, keepdims=True)
        lrun[...] = jnp.zeros((8, ROWS), F32)

        def sum_step(b, carry):
            lrun[...] += jnp.sum(jnp.exp(scores[b] - top).reshape(KEYS // 8, 8, ROWS), axis=0)
            return carry

        lax.fori_loop(0, last + 1, sum_step, 0)
        stat[...] = top + jnp.log(jnp.sum(lrun[...], axis=0, keepdims=True))
        dqt[...] = jnp.zeros((128, ROWS), F32)

    def gather_hidden(h):
        hsum = hown[h]
        for xrel in (1, 3, 2):
            xr_copy(h, xrel).wait_recv()
            hsum = hsum + xrecv[h, xrel - 1].astype(F32)
        hidg[h, c, x] = hsum.astype(BF16)
        for xrel in (2, 1, 3):
            xg_copy(h, x, xrel).start()
        cg_copy(h, x, c).start()

    def terms(h):
        for xrel in (1, 3, 2):
            xx = (x - xrel + NX) % NX
            xg_copy(h, xx, xrel).wait_recv()
            cg_copy(h, xx, c).start()
        slot_terms(h, c)
        for xx in range(NX):
            cg_copy(h, xx, 1 - c).wait_recv()
        slot_terms(h, 1 - c)

    def row_grads(yrel):
        @pl.when(y >= yrel)
        def _():
            def v_wait(zz, carry):
                kvy_copy(vg, 1, y - yrel, yrel, zz).wait_recv()
                return carry

            if yrel == 2:
                kv2_wait(1)
            else:
                lax.fori_loop(0, NZ, v_wait, 0)

            def row_step(turn, carry):
                blk = (z // 2 + 1 + turn) % PAIRS
                grad_block((y - yrel) * PAIRS + blk)
                if yrel == 2:
                    for i in range(2):
                        zz = 2 * blk + i

                        @pl.when(zz != z)
                        def _():
                            d2z_copy(z, zz).start()

                else:
                    dy_copy(yrel, y - yrel, blk).start()
                return carry

            lax.fori_loop(0, PAIRS, row_step, 0)

    def combine(n):
        for yrel in y_order:
            ysrc = (y - yrel + NY) % NY
            remote(
                tsend.at[y, n], trecv.at[n, :, ysrc], t_s.at[n, yrel - 1], t_r.at[n, yrel - 1], y_dev(ysrc)
            ).wait_recv()

        for j in (2, 1, 3, 0):
            pair = (z // 2 + j) % PAIRS
            tokens = dot(tables[pair], trecv[n, pair].reshape(ROW_SLOTS, HALF_COLS), NN)
            for i in range(2):
                zz = pair * 2 + i
                part = tokens[i * TOK:(i + 1) * TOK]

                @pl.when(zz == z)
                def _():
                    mown[n] = part

                @pl.when(zz != z)
                def _():
                    zsend[n, zz] = part.astype(BF16)
                    tz_copy(n, z, zz).start()

    def own_grads():
        def own_step(blk, carry):
            b = y * PAIRS + blk

            @pl.when(b <= last)
            def _():
                grad_block(b)

            @pl.when(b > last)
            def _():
                dkv[pl.ds(2 * b, 2)] = jnp.zeros((2, ATT, 256), BF16)

            return carry

        lax.fori_loop(0, PAIRS, own_step, 0)
        for g in range(GROUP):
            cols = slice(g * 128, (g + 1) * 128)
            dq_ref[:, cols] = dqt[:, cols].T.astype(BF16)

    def dz_copy(zsrc, zdst):
        return remote(dzsend.at[zdst], dzrecv.at[zsrc], dz_s.at[zdst], dz_r.at[zsrc], z_dev(zdst))

    def dz_needed(zsrc, zdst):
        return (y < NY - 1) | (zdst < zsrc)

    def spread():
        def pair_step(turn, carry):
            blk = (z // 2 + 1 + turn) % PAIRS
            for yrel in (1, 3):

                @pl.when(y + yrel < NY)
                def _():
                    dst = drecv.at[yrel - 1, pl.ds(2 * blk, 2)]
                    remote(
                        dst, dst, dy_s.at[yrel - 1, blk], dy_r.at[yrel - 1, blk], y_dev((y + yrel) % NY)
                    ).wait_recv()

            for i in range(2):
                zz = 2 * blk + (z + 1 + i) % 2
                dtmp[...] = dkv[y * NZ + zz].astype(F32)
                for yrel in (1, 3):

                    @pl.when(y + yrel < NY)
                    def _():
                        dtmp[...] += drecv[yrel - 1, zz].astype(F32)

                @pl.when((zz != z) & dz_needed(z, zz))
                def _():
                    dzsend[zz] = dtmp[...].astype(BF16)
                    dz_copy(z, zz).start()

            return carry

        lax.fori_loop(0, PAIRS, pair_step, 0)
        down[...] = dtmp[...]

    turn_gate()
    dispatch()
    for n in (5, 6):
        loads[n].wait()
    send_kv()
    turn_up()
    prepare()
    loads[0].wait()
    slots_wait(1)
    slots_wait(2)
    hidden_other(0)
    hidden_mine(0)
    slots_wait(3)
    hidden_other(1)
    hidden_sum(0)
    hidden_mine(1)
    hidden_sum(1)
    kv2_on(0)
    kv2_on(1)
    kv_on(0)
    kv_on(1)
    own_scores()
    gather_hidden(0)
    gather_hidden(1)
    for yrel in (1, 3, 2):
        row_scores(yrel)
    totals()
    loads[3].wait()
    loads[4].wait()
    terms(0)
    terms(1)
    for yrel in (2, 3, 1):
        row_grads(yrel)
    combine(0)
    combine(1)
    row_sum()
    own_grads()
    spread()

    for n in range(2):
        cols = slice(n * HALF_COLS, (n + 1) * HALF_COLS)
        acc = mown[n] + upper_ref[:, cols].astype(F32)
        for k in z_order:
            zz = (z + k) % NZ
            tz_copy(n, zz, z).wait_recv()
            acc = acc + zrecv[n, zz].astype(F32)
        moe_ref[:, cols] = acc.astype(BF16)

    for k in z_order:
        zz = (z + k) % NZ

        @pl.when(dz_needed(zz, z))
        def _():
            dz_copy(zz, z).wait_recv()
            down[...] += dzrecv[zz].astype(F32)

    @pl.when(y < 2)
    def _():
        d2y_copy(y).wait_recv()
        down[...] += d2in[...].astype(F32)

    dk_ref[...] = down[:, 0:128].astype(BF16)
    dv_ref[...] = down[:, 128:256].astype(BF16)

    for k in z_order:
        zz = (z + k) % NZ
        up_copy(z, zz).wait_send()
        meta_copy(z, zz).wait_send()
        tz_copy(0, z, zz).wait_send()
        tz_copy(1, z, zz).wait_send()

        @pl.when(kvz_needed(z, zz))
        def _():
            kvz_copy(kg, 0, z, zz).wait_send()
            kvz_copy(vg, 1, z, zz).wait_send()

        @pl.when(dz_needed(z, zz))
        def _():
            dz_copy(z, zz).wait_send()

        @pl.when(y >= 2)
        def _():
            kv2z_copy(kg, 0, z, zz).wait_send()
            kv2z_copy(vg, 1, z, zz).wait_send()
            d2z_copy(z, zz).wait_send()

    @pl.when(y >= 2)
    def _():
        d2y_copy((y + 2) % NY).wait_send()

    @pl.when(y < 2)
    def _():
        kv2y_copy(kg, 0, y).wait_send()
        kv2y_copy(vg, 1, y).wait_send()

    for yrel in range(1, NY):
        for pair in range(PAIRS):
            slot_copy(yrel, pair).wait_send()
        t_copy(0, yrel).wait_send()
        t_copy(1, yrel).wait_send()

    for yrel in (1, 3):

        @pl.when(y + yrel < NY)
        def _():
            def kvy_sent(zz, carry):
                kvy_copy(kg, 0, y, yrel, zz).wait_send()
                kvy_copy(vg, 1, y, yrel, zz).wait_send()
                return carry

            lax.fori_loop(0, NZ, kvy_sent, 0)

        @pl.when(y >= yrel)
        def _():
            def dy_sent(blk, carry):
                dy_copy(yrel, y - yrel, blk).wait_send()
                return carry

            lax.fori_loop(0, PAIRS, dy_sent, 0)

    for h in range(2):
        core_copy(h).wait_send()
        for xrel in range(1, NX):
            xr_copy(h, xrel).wait_send()
            xg_copy(h, x, xrel).wait_send()
        for xx in range(NX):
            cg_copy(h, xx, c).wait_send()


def vmem(*shape, dtype=BF16):
    return pltpu.VMEM(shape, dtype)


def copy_kernel(*refs):
    for i in range(4):
        refs[4 + i][...] = refs[i][...]


def on_device(upper, ids, slots, probs, gate_pre, up_pre, w_gate, w_up, *rest):
    args = (upper, ids.T, slots.T, probs.T) + tuple(jnp.swapaxes(a, 1, 2) for a in (gate_pre, up_pre, w_gate, w_up)) + rest
    dma = pltpu.SemaphoreType.DMA
    whole = pl.BlockSpec(memory_space=pltpu.VMEM)
    anywhere = pl.BlockSpec(memory_space=pl.ANY)
    outs = [(TOK, COLS), (ATT, COLS), (ATT, HEAD_DIM), (ATT, HEAD_DIM)]
    out_shape = [jax.ShapeDtypeStruct(shape, BF16) for shape in outs]
    grads = pl.pallas_call(
        kernel,
        out_shape=out_shape,
        in_specs=[whole] * 4 + [anywhere] * 10,
        out_specs=[whole] * 4,
        scratch_shapes=[
            vmem(COLS, UNITS), vmem(COLS, UNITS), vmem(UNITS, COLS), vmem(UNITS, COLS),
            vmem(UNITS, COLS), vmem(UNITS, COLS), vmem(UNITS, COLS), vmem(ATT, COLS), vmem(ATT, COLS), vmem(ATT, COLS), dma((10,)),
            vmem(NZ, TOK, COLS), vmem(NZ, TOK, 128, dtype=F32), vmem(8 * TOK, COLS), vmem(8 * TOK, ROW_SLOTS),
            vmem(PAIRS, 2 * TOK, ROW_SLOTS), vmem(NY, ROW_SLOTS, COLS), vmem(NY, ROW_SLOTS, COLS),
            vmem(2, ROW_SLOTS, UNITS, dtype=F32), vmem(2, ROW_SLOTS, UNITS), vmem(2, ROW_SLOTS, UNITS),
            vmem(2, NX, PAIR_SLOTS, UNITS), vmem(2, NX - 1, PAIR_SLOTS, UNITS), vmem(2, PAIR_SLOTS, UNITS, dtype=F32),
            vmem(2, NC, NX, PAIR_SLOTS, UNITS),
            vmem(NY, 2, PAIRS, PAIR_SLOTS, HALF_COLS), vmem(2, PAIRS, NY, PAIR_SLOTS, HALF_COLS),
            vmem(2, NZ, TOK, HALF_COLS), vmem(2, NZ, TOK, HALF_COLS), vmem(2, TOK, HALF_COLS, dtype=F32),
            vmem(NY * NZ, ATT, 128), vmem(NY * NZ, ATT, 128), vmem(ROWS, 128), vmem(ROWS, 128), vmem(1, ROWS, dtype=F32),
            vmem(BLOCKS, KEYS, ROWS, dtype=F32), vmem(8, ROWS, dtype=F32), vmem(8, ROWS, dtype=F32), vmem(1, ROWS, dtype=F32),
            vmem(128, ROWS, dtype=F32), vmem(NY * NZ, ATT, 256), vmem(NY - 1, NZ, ATT, 256), vmem(NZ, ATT, 256), vmem(ATT, 256), vmem(ATT, 256),
            vmem(NZ, ATT, 256), vmem(NZ, ATT, 256), vmem(ATT, 256, dtype=F32), vmem(ATT, 256, dtype=F32),
            dma((NZ,)), dma((NZ,)), dma((NZ,)), dma((NZ,)), dma((2, NZ)), dma((2, NZ)),
            dma((2, NY - 1, NZ)), dma((2, NY - 1, NZ)), dma((NY - 1, PAIRS)), dma((NY - 1, PAIRS)),
            dma((2,)), dma((2,)), dma((2, NX - 1)), dma((2, NX - 1)), dma((2, NX - 1)), dma((2, NX - 1)),
            dma((2, NX)), dma((2, NX)),
            dma((2, NY - 1)), dma((2, NY - 1)), dma((2, NZ)), dma((2, NZ)),
            dma((NY - 1, PAIRS)), dma((NY - 1, PAIRS)), dma((NZ,)), dma((NZ,)),
            dma((2,)), dma((2,)), dma((2, NZ)), dma((2, NZ)), dma((NZ,)), dma((NZ,)), dma((1,)), dma((1,)),
        ],
        compiler_params=pltpu.CompilerParams(
            collective_id=0, has_side_effects=True, vmem_limit_bytes=60 * 1024 * 1024
        ),
        cost_estimate=pl.CostEstimate(flops=9_000_000_000, bytes_accessed=14_000_000, transcendentals=8_000_000),
        name="layer_grad",
    )(*args)
    return pl.pallas_call(
        copy_kernel,
        out_shape=out_shape,
        in_specs=[whole] * 4,
        out_specs=[whole] * 4,
        name="hand_out",
    )(*grads)


def solution(mesh):
    return jax.shard_map(
        on_device,
        mesh=mesh,
        in_specs=(
            P("expert", "pipe"),
            P("expert", None),
            P("expert", None),
            P("expert", None),
            P("expert", None, None),
            P("expert", None, None),
            P("expert", "pipe", None),
            P("expert", "pipe", None),
            P("expert", None, "pipe"),
            P("expert", "pipe"),
            P("expert", "pipe"),
            P("expert", "pipe"),
            P("expert", "pipe"),
            P("expert", "pipe"),
        ),
        out_specs=(
            P("expert", "pipe"),
            P("expert", "pipe"),
            P("expert", "pipe"),
            P("expert", "pipe"),
        ),
        check_vma=False,
    )
```

```python
import math

import jax
import jax.numpy as jnp
from jax import lax
from jax.experimental import pallas as pl
from jax.experimental.pallas import tpu as pltpu
from jax.sharding import PartitionSpec as P

MESH = pl.DeviceIdType.MESH
F32 = jnp.float32
BF16 = jnp.bfloat16

EXPERTS = 8
HEAD_DIM = 128
GROUP = 6
TOK = 32
ATT = 128
CAP = 24
UNITS = 1344
COLS = 768
HALF_COLS = COLS // 2
ROWS = GROUP * ATT
NX, NC, NY, NZ = 4, 2, 4, 8
PAIRS = NZ // 2
PAIR_SLOTS = 2 * CAP
ROW_SLOTS = NZ * CAP
KEYS = 2 * ATT
WIDE = 2
BLOCKS = NY * PAIRS
SCALE = HEAD_DIM ** (-0.5)
SCALE_BITS = SCALE * math.log2(math.e)
MASKED = -1e30

NT = (((1,), (1,)), ((), ()))
TN = (((0,), (0,)), ((), ()))
NN = (((1,), (0,)), ((), ()))


def dot(a, b, dims):
    return lax.dot_general(a, b, dims, preferred_element_type=F32)


def kernel(
    upper_ref, ids_ref, slot_ref, prob_ref, gpre_hbm, upre_hbm, wg_hbm, wu_hbm, wd_hbm,
    q_hbm, k_hbm, v_hbm, o_hbm, do_hbm,
    moe_ref, dq_ref, dk_ref, dv_ref,
    gpre, upre, gpre_t, upre_t, wg, wu, wd, q_ref, o_ref, do_ref, load_sem,
    upg, metag, stack, picks, tables, sbuf, arrived,
    hpart, csend, crecv, xsend, xrecv, hown, hidg,
    tsend, trecv, zsend, zrecv, mown,
    kg, vg, qrows, dorows, delta, scores, mrun, lrun, stat, dqt, dkv, drecv, d2recv, d2sum, d2in, dzsend, dzrecv, dtmp, down,
    up_s, up_r, meta_s, meta_r, kvz_s, kvz_r, kvy_s, kvy_r, sl_s, sl_r,
    core_s, core_r, xr_s, xr_r, xg_s, xg_r, cg_s, cg_r, t_s, t_r, tz_s, tz_r,
    dy_s, dy_r, dz_s, dz_r, kv2y_s, kv2y_r, kv2z_s, kv2z_r, d2z_s, d2z_r, d2y_s, d2y_r,
):
    p = lax.axis_index("pipe")
    e = lax.axis_index("expert")
    x, c = p // NC, p % NC
    y, z = e // NZ, e % NZ
    half = z // 4

    def at(xx, cc, yy, zz):
        return (xx * NC + cc, yy * NZ + zz)

    def z_dev(zz):
        return at(x, c, y, zz)

    def y_dev(yy):
        return at(x, c, yy, z)

    def x_dev(xx):
        return at(xx, c, y, z)

    core_dev = at(x, 1 - c, y, z)

    def remote(src, dst, ss, rs, dev):
        return pltpu.make_async_remote_copy(
            src_ref=src, dst_ref=dst, send_sem=ss, recv_sem=rs, device_id=dev, device_id_type=MESH
        )

    loads = [
        pltpu.make_async_copy(src, dst, load_sem.at[i])
        for i, (src, dst) in enumerate(
            (
                (wd_hbm.at[0], wd), (gpre_hbm.at[0], gpre_t), (upre_hbm.at[0], upre_t), (wg_hbm.at[0], wg), (wu_hbm.at[0], wu),
                (k_hbm, kg.at[e]), (v_hbm, vg.at[e]), (q_hbm, q_ref), (o_hbm, o_ref), (do_hbm, do_ref),
            )
        )
    ]

    upg[z] = upper_ref[...]
    kept = slot_ref[...] >= 0
    dtmp[...] = jnp.zeros((ATT, 256), F32)
    dtmp[0:4, 0:TOK] = jnp.where(kept, ids_ref[...] * CAP + slot_ref[...], -1).astype(F32)
    dtmp[4:8, 0:TOK] = prob_ref[...]
    metag[z] = dtmp[0:8, 0:128]

    barrier = pltpu.get_barrier_semaphore()
    peers = (
        [z_dev((z + k) % NZ) for k in range(1, NZ)]
        + [y_dev((y + k) % NY) for k in range(1, NY)]
        + [x_dev((x + k) % NX) for k in range(1, NX)]
        + [core_dev]
    )
    for peer in peers:
        pl.semaphore_signal(barrier, inc=1, device_id=peer, device_id_type=MESH)
    pl.semaphore_wait(barrier, len(peers))

    z_order = (1, 7, 2, 6, 3, 5, 4)
    y_order = (1, 3, 2)

    def up_copy(zsrc, zdst):
        return remote(upg.at[zsrc], upg.at[zsrc], up_s.at[zdst], up_r.at[zsrc], z_dev(zdst))

    def meta_copy(zsrc, zdst):
        return remote(metag.at[zsrc], metag.at[zsrc], meta_s.at[zdst], meta_r.at[zsrc], z_dev(zdst))

    def kvz_needed(zsrc, zdst):
        return (y < NY - 1) | (zdst // 2 >= zsrc // 2)

    def kv2y_copy(buf, n, ysrc):
        blk = buf.at[ysrc * NZ + z]
        return remote(blk, blk, kv2y_s.at[n], kv2y_r.at[n], y_dev((ysrc + 2) % NY))

    def kv2z_copy(buf, n, zsrc, zdst):
        blk = buf.at[(y - 2) * NZ + zsrc]
        return remote(blk, blk, kv2z_s.at[n, zdst], kv2z_r.at[n, zsrc], z_dev(zdst))

    def kvz_copy(buf, n, zsrc, zdst):
        blk = buf.at[y * NZ + zsrc]
        return remote(blk, blk, kvz_s.at[n, zdst], kvz_r.at[n, zsrc], z_dev(zdst))

    for k in z_order:
        up_copy(z, (z + k) % NZ).start()
        meta_copy(z, (z + k) % NZ).start()
    col = lax.broadcasted_iota(jnp.int32, (TOK, 4 * PAIR_SLOTS), 1)
    col_y = (
        (col >= PAIR_SLOTS).astype(jnp.int32)
        + (col >= 2 * PAIR_SLOTS).astype(jnp.int32)
        + (col >= 3 * PAIR_SLOTS).astype(jnp.int32)
    )
    col_in = col - PAIR_SLOTS * col_y
    col_i = (col_in >= CAP).astype(jnp.int32)
    wanted = (2 * col_y + half) * CAP + (col_in - CAP * col_i)

    def slot_copy(yrel, pair):
        ydst = (y + yrel) % NY
        rows = pl.ds(pl.multiple_of(pair * PAIR_SLOTS, 16), PAIR_SLOTS)
        return remote(
            sbuf.at[ydst, rows], arrived.at[y, rows], sl_s.at[yrel - 1, pair], sl_r.at[yrel - 1, pair], y_dev(ydst)
        )

    sources = ((1, 2), (3, 0))

    def source_row(h, cc):
        return (y + NY - jnp.where(cc == 0, sources[h][0], sources[h][1])) % NY

    def core_copy(h):
        return remote(csend.at[h], crecv.at[h], core_s.at[h], core_r.at[h], core_dev)

    def xr_copy(h, xrel):
        xdst = (x + xrel) % NX
        return remote(
            xsend.at[h, xdst], xrecv.at[h, xrel - 1], xr_s.at[h, xrel - 1], xr_r.at[h, xrel - 1], x_dev(xdst)
        )

    def slots_wait(yrel):
        ysrc = (y - yrel + NY) % NY
        for pair in range(PAIRS):
            rows = pl.ds(pair * PAIR_SLOTS, PAIR_SLOTS)
            remote(
                sbuf.at[ysrc, rows], arrived.at[ysrc, rows], sl_s.at[yrel - 1, pair], sl_r.at[yrel - 1, pair], y_dev(ysrc)
            ).wait_recv()

    def hidden_other(h):
        csend[h] = dot(arrived[source_row(h, 1 - c)], wd[...], NT).astype(BF16)
        core_copy(h).start()

    def hidden_mine(h):
        hpart[h] = dot(arrived[source_row(h, c)], wd[...], NT)

    def hidden_sum(h):
        core_copy(h).wait_recv()
        for xrel in (2, 1, 3, 0):
            xx = (x + xrel) % NX
            rows = pl.ds(pl.multiple_of(xx * PAIR_SLOTS, 16), PAIR_SLOTS)
            total = hpart[h, rows] + crecv[h, rows].astype(F32)
            if xrel > 0:
                xsend[h, xx] = total.astype(BF16)
                xr_copy(h, xrel).start()
            else:
                hown[h] = total

    def kvy_copy(buf, n, ysrc, yrel, zz):
        blk = buf.at[ysrc * NZ + zz]
        return remote(blk, blk, kvy_s.at[n, yrel - 1, zz], kvy_r.at[n, yrel - 1, zz], y_dev((ysrc + yrel) % NY))

    def kv_on(n):
        buf = (kg, vg)[n]

        def kv_forward(k, carry):
            zz = (z + k) % NZ

            @pl.when((k > 0) & kvz_needed(zz, z))
            def _():
                kvz_copy(buf, n, zz, z).wait_recv()

            for yrel in (1, 3):

                @pl.when(y + yrel < NY)
                def _():
                    kvy_copy(buf, n, y, yrel, zz).start()

            return carry

        lax.fori_loop(0, NZ, kv_forward, 0)

    def score_block(b, count, masked):
        keys = kg[pl.ds(2 * b, 2 * count)].reshape(count * KEYS, 128)
        s = dot(keys, qrows[...], NT) * SCALE_BITS
        if masked:
            key_pos = b * KEYS + lax.broadcasted_iota(jnp.int32, (KEYS, ROWS), 0)
            row_pos = e * ATT + (lax.broadcasted_iota(jnp.int32, (KEYS, ROWS), 1) & 127)
            s = jnp.where(key_pos <= row_pos, s, MASKED)
        scores[pl.ds(b, count)] = s.reshape(count, KEYS, ROWS)
        mrun[...] = jnp.maximum(mrun[...], jnp.max(s.reshape(count * KEYS // 8, 8, ROWS), axis=0))

    def score_step(b, carry):
        score_block(b, 1, False)
        return carry

    last = e // 2

    def xg_copy(h, xsrc, xrel):
        blk = hidg.at[h, c, xsrc]
        return remote(blk, blk, xg_s.at[h, xrel - 1], xg_r.at[h, xrel - 1], x_dev((xsrc + xrel) % NX))

    def cg_copy(h, xx, cc):
        blk = hidg.at[h, cc, xx]
        return remote(blk, blk, cg_s.at[h, xx], cg_r.at[h, xx], core_dev)

    def t_copy(n, yrel):
        ydst = (y + yrel) % NY
        return remote(tsend.at[ydst, n], trecv.at[n, :, y], t_s.at[n, yrel - 1], t_r.at[n, yrel - 1], y_dev(ydst))

    def slot_terms(h, cc):
        ysrc = source_row(h, cc)
        rows = pl.ds(pl.multiple_of(ysrc * ROW_SLOTS, 16), ROW_SLOTS)
        hid = hidg[h, cc].reshape(ROW_SLOTS, UNITS).astype(F32)
        a = gpre[rows, :].astype(F32)
        b = upre[rows, :].astype(F32)
        s = 1.0 / (1.0 + jnp.exp(-a))
        hs = hid * s
        gate_grad = (hs * b * (1.0 + a * (1.0 - s))).astype(BF16)
        up_grad = (hs * a).astype(BF16)
        rel = (ysrc - y + NY) % NY
        for n in range(2):
            cols = slice(n * HALF_COLS, (n + 1) * HALF_COLS)
            part = dot(gate_grad, wg[:, cols], NN) + dot(up_grad, wu[:, cols], NN)
            tsend[ysrc, n] = part.astype(BF16).reshape(PAIRS, PAIR_SLOTS, HALF_COLS)

            @pl.when(rel == 0)
            def _():
                trecv[n, :, y] = tsend[y, n]

            @pl.when(rel > 0)
            def _():
                t_copy(n, rel).start()

    def grad_block(b, count):
        size = count * KEYS
        keys = kg[pl.ds(2 * b, 2 * count)].reshape(size, 128)
        values = vg[pl.ds(2 * b, 2 * count)].reshape(size, 128)
        probs = jnp.exp2(scores[pl.ds(b, count)].reshape(size, ROWS) - stat[...])
        grad_probs = dot(values, dorows[...], NT)
        ds = (probs * (grad_probs - delta[...])).astype(BF16)
        dqt[...] += dot(keys, ds, TN)
        key_grad = (dot(ds, qrows[...], NN) * SCALE).astype(BF16)
        value_grad = dot(probs.astype(BF16), dorows[...], NN).astype(BF16)
        dkv[pl.ds(2 * b, 2 * count), :, 0:128] = key_grad.reshape(2 * count, ATT, 128)
        dkv[pl.ds(2 * b, 2 * count), :, 128:256] = value_grad.reshape(2 * count, ATT, 128)

    def dy_copy(yrel, ydst, blk):
        src = dkv.at[pl.ds(ydst * NZ + 2 * blk, 2)]
        return remote(src, drecv.at[yrel - 1, pl.ds(2 * blk, 2)], dy_s.at[yrel - 1, blk], dy_r.at[yrel - 1, blk], y_dev(ydst))

    def d2z_copy(zsrc, zdst):
        return remote(
            dkv.at[(y - 2) * NZ + zdst], d2recv.at[zsrc], d2z_s.at[zdst], d2z_r.at[zsrc], z_dev(zdst)
        )

    def d2y_copy(ydst):
        return remote(d2sum, d2in, d2y_s.at[0], d2y_r.at[0], y_dev(ydst))

    def row_sum():
        @pl.when(y >= 2)
        def _():
            dtmp[...] = dkv[(y - 2) * NZ + z].astype(F32)
            for k in z_order:
                zz = (z + k) % NZ
                d2z_copy(zz, z).wait_recv()
                dtmp[...] += d2recv[zz].astype(F32)
            d2sum[...] = dtmp[...].astype(BF16)
            d2y_copy((y + 2) % NY).start()

    def tz_copy(n, zsrc, zdst):
        return remote(zsend.at[n, zdst], zrecv.at[n, zsrc], tz_s.at[n, zdst], tz_r.at[n, zsrc], z_dev(zdst))

    def send_kv():
        for n, buf in enumerate((kg, vg)):

            @pl.when(y < 2)
            def _():
                kv2y_copy(buf, n, y).start()

        for n, buf in enumerate((kg, vg)):
            for k in z_order:
                zdst = (z + k) % NZ

                @pl.when(kvz_needed(z, zdst))
                def _():
                    kvz_copy(buf, n, z, zdst).start()

    def kv2_on(n):
        buf = (kg, vg)[n]

        @pl.when(y >= 2)
        def _():
            kv2y_copy(buf, n, y - 2).wait_recv()
            for k in z_order:
                kv2z_copy(buf, n, z, (z + k) % NZ).start()

    def kv2_wait(n):
        for k in z_order:
            kv2z_copy((kg, vg)[n], n, (z + k) % NZ, z).wait_recv()

    def turn_gate():
        loads[1].wait()
        for i in range(COLS // 128):
            cols = slice(i * 128, (i + 1) * 128)
            gpre[cols, :] = gpre_t[:, cols].T

    def turn_up():
        loads[2].wait()
        for i in range(COLS // 128):
            cols = slice(i * 128, (i + 1) * 128)
            upre[cols, :] = upre_t[:, cols].T

    def prepare():
        for n in (7, 8, 9):
            loads[n].wait()
        for g in range(GROUP):
            cols = slice(g * 128, (g + 1) * 128)
            qrows[g * 128:(g + 1) * 128, :] = q_ref[:, cols]
            dorows[g * 128:(g + 1) * 128, :] = do_ref[:, cols]
            prod = do_ref[:, cols].astype(F32) * o_ref[:, cols].astype(F32)
            delta[:, cols] = jnp.sum(prod.T, axis=0, keepdims=True)

    def dispatch(turns):
        for j in turns:
            pair = (z // 2 + j) % PAIRS
            for i in range(2):
                zz = pair * 2 + i

                @pl.when(zz != z)
                def _():
                    up_copy(zz, z).wait_recv()
                    meta_copy(zz, z).wait_recv()

                meta = metag[zz].T[0:TOK]
                tokens = upg[zz].astype(F32)
                target = meta[:, 0:4].astype(jnp.int32)
                mine = jnp.where(col_i == i, wanted, -2)
                table = jnp.zeros((TOK, 4 * PAIR_SLOTS), F32)
                for k in range(4):
                    row = (i * 4 + k) * TOK
                    stack[row:row + TOK, :] = (meta[:, 4 + k:5 + k] * tokens).astype(BF16)
                    hit = (target[:, k:k + 1] == mine).astype(F32)
                    table = table + hit
                    picks[row:row + TOK, :] = hit.astype(BF16)
                tables[pair, i * TOK:(i + 1) * TOK, :] = table.astype(BF16)
            picked = dot(picks[...], stack[...], TN).astype(BF16)
            rows = pl.ds(pl.multiple_of(pair * PAIR_SLOTS, 16), PAIR_SLOTS)
            for yy in range(NY):
                sbuf[yy, rows, :] = picked[yy * PAIR_SLOTS:(yy + 1) * PAIR_SLOTS]
            arrived[y, rows, :] = sbuf[y, rows, :]
            for yrel in y_order:
                slot_copy(yrel, pair).start()

    def own_scores():
        mrun[...] = jnp.full((8, ROWS), MASKED, F32)
        score_block(last, 1, True)
        lax.fori_loop(y * PAIRS, last, score_step, 0)

    def row_scores(yrel):
        @pl.when(y >= yrel)
        def _():
            ysrc = y - yrel

            def k_wait(zz, carry):
                kvy_copy(kg, 0, ysrc, yrel, zz).wait_recv()
                return carry

            if yrel == 2:
                kv2_wait(0)
            else:
                lax.fori_loop(0, NZ, k_wait, 0)

            def wide_step(i, carry):
                score_block(ysrc * PAIRS + WIDE * i, WIDE, False)
                return carry

            lax.fori_loop(0, PAIRS // WIDE, wide_step, 0)

    def totals():
        top = jnp.max(mrun[...], axis=0, keepdims=True)
        lrun[...] = jnp.zeros((8, ROWS), F32)

        def sum_step(b, carry):
            lrun[...] += jnp.sum(jnp.exp2(scores[b] - top).reshape(KEYS // 8, 8, ROWS), axis=0)
            return carry

        lax.fori_loop(0, last + 1, sum_step, 0)
        stat[...] = top + jnp.log2(jnp.sum(lrun[...], axis=0, keepdims=True))
        dqt[...] = jnp.zeros((128, ROWS), F32)

    def gather_hidden(h):
        hsum = hown[h]
        for xrel in (1, 3, 2):
            xr_copy(h, xrel).wait_recv()
            hsum = hsum + xrecv[h, xrel - 1].astype(F32)
        hidg[h, c, x] = hsum.astype(BF16)
        for xrel in (2, 1, 3):
            xg_copy(h, x, xrel).start()
        cg_copy(h, x, c).start()

    def terms(h):
        for xrel in (1, 3, 2):
            xx = (x - xrel + NX) % NX
            xg_copy(h, xx, xrel).wait_recv()
            cg_copy(h, xx, c).start()
        slot_terms(h, c)
        for xx in range(NX):
            cg_copy(h, xx, 1 - c).wait_recv()
        slot_terms(h, 1 - c)

    def row_grads(yrel):
        @pl.when(y >= yrel)
        def _():
            def v_wait(zz, carry):
                kvy_copy(vg, 1, y - yrel, yrel, zz).wait_recv()
                return carry

            if yrel == 2:
                kv2_wait(1)
            else:
                lax.fori_loop(0, NZ, v_wait, 0)

            def row_step(turn, carry):
                first = (z // 2 + WIDE * (turn + 1)) % PAIRS // WIDE * WIDE
                grad_block((y - yrel) * PAIRS + first, WIDE)
                for i in range(WIDE):
                    if yrel == 2:
                        for j in range(2):
                            zz = 2 * (first + i) + j

                            @pl.when(zz != z)
                            def _():
                                d2z_copy(z, zz).start()

                    else:
                        dy_copy(yrel, y - yrel, first + i).start()
                return carry

            lax.fori_loop(0, PAIRS // WIDE, row_step, 0)

    def combine(n):
        for yrel in y_order:
            ysrc = (y - yrel + NY) % NY
            remote(
                tsend.at[y, n], trecv.at[n, :, ysrc], t_s.at[n, yrel - 1], t_r.at[n, yrel - 1], y_dev(ysrc)
            ).wait_recv()

        for j in (2, 1, 3, 0):
            pair = (z // 2 + j) % PAIRS
            tokens = dot(tables[pair], trecv[n, pair].reshape(ROW_SLOTS, HALF_COLS), NN)
            for i in range(2):
                zz = pair * 2 + i
                part = tokens[i * TOK:(i + 1) * TOK]

                @pl.when(zz == z)
                def _():
                    mown[n] = part

                @pl.when(zz != z)
                def _():
                    zsend[n, zz] = part.astype(BF16)
                    tz_copy(n, z, zz).start()

    def own_grads():
        def own_step(blk, carry):
            b = y * PAIRS + blk

            @pl.when(b <= last)
            def _():
                grad_block(b, 1)

            @pl.when(b > last)
            def _():
                dkv[pl.ds(2 * b, 2)] = jnp.zeros((2, ATT, 256), BF16)

            return carry

        lax.fori_loop(0, PAIRS, own_step, 0)
        for g in range(GROUP):
            cols = slice(g * 128, (g + 1) * 128)
            dq_ref[:, cols] = (dqt[:, cols].T * SCALE).astype(BF16)

    def dz_copy(zsrc, zdst):
        return remote(dzsend.at[zdst], dzrecv.at[zsrc], dz_s.at[zdst], dz_r.at[zsrc], z_dev(zdst))

    def dz_needed(zsrc, zdst):
        return (y < NY - 1) | (zdst < zsrc)

    def spread():
        def pair_step(turn, carry):
            blk = (z // 2 + 1 + turn) % PAIRS
            for yrel in (1, 3):

                @pl.when(y + yrel < NY)
                def _():
                    dst = drecv.at[yrel - 1, pl.ds(2 * blk, 2)]
                    remote(
                        dst, dst, dy_s.at[yrel - 1, blk], dy_r.at[yrel - 1, blk], y_dev((y + yrel) % NY)
                    ).wait_recv()

            for i in range(2):
                zz = 2 * blk + (z + 1 + i) % 2
                dtmp[...] = dkv[y * NZ + zz].astype(F32)
                for yrel in (1, 3):

                    @pl.when(y + yrel < NY)
                    def _():
                        dtmp[...] += drecv[yrel - 1, zz].astype(F32)

                @pl.when((zz != z) & dz_needed(z, zz))
                def _():
                    dzsend[zz] = dtmp[...].astype(BF16)
                    dz_copy(z, zz).start()

            return carry

        lax.fori_loop(0, PAIRS, pair_step, 0)
        down[...] = dtmp[...]

    def start(*which):
        for n in which:
            loads[n].start()

    start(5, 6, 1, 2, 0, 7, 9, 8, 3, 4)
    turn_gate()
    dispatch((0, 1, 3, 2))
    for n in (5, 6):
        loads[n].wait()
    send_kv()
    turn_up()
    prepare()
    loads[0].wait()
    slots_wait(1)
    slots_wait(2)
    hidden_other(0)
    hidden_mine(0)
    slots_wait(3)
    hidden_other(1)
    hidden_sum(0)
    hidden_mine(1)
    hidden_sum(1)
    kv2_on(0)
    kv2_on(1)
    kv_on(0)
    kv_on(1)
    own_scores()
    gather_hidden(0)
    gather_hidden(1)
    for yrel in (1, 3, 2):
        row_scores(yrel)
    totals()
    loads[3].wait()
    loads[4].wait()
    terms(0)
    terms(1)
    for yrel in (2, 3, 1):
        row_grads(yrel)
    combine(0)
    combine(1)
    row_sum()
    own_grads()
    spread()

    for n in range(2):
        cols = slice(n * HALF_COLS, (n + 1) * HALF_COLS)
        acc = mown[n] + upper_ref[:, cols].astype(F32)
        for k in z_order:
            zz = (z + k) % NZ
            tz_copy(n, zz, z).wait_recv()
            acc = acc + zrecv[n, zz].astype(F32)
        moe_ref[:, cols] = acc.astype(BF16)

    for k in z_order:
        zz = (z + k) % NZ

        @pl.when(dz_needed(zz, z))
        def _():
            dz_copy(zz, z).wait_recv()
            down[...] += dzrecv[zz].astype(F32)

    @pl.when(y < 2)
    def _():
        d2y_copy(y).wait_recv()
        down[...] += d2in[...].astype(F32)

    dk_ref[...] = down[:, 0:128].astype(BF16)
    dv_ref[...] = down[:, 128:256].astype(BF16)

    for k in z_order:
        zz = (z + k) % NZ
        up_copy(z, zz).wait_send()
        meta_copy(z, zz).wait_send()
        tz_copy(0, z, zz).wait_send()
        tz_copy(1, z, zz).wait_send()

        @pl.when(kvz_needed(z, zz))
        def _():
            kvz_copy(kg, 0, z, zz).wait_send()
            kvz_copy(vg, 1, z, zz).wait_send()

        @pl.when(dz_needed(z, zz))
        def _():
            dz_copy(z, zz).wait_send()

        @pl.when(y >= 2)
        def _():
            kv2z_copy(kg, 0, z, zz).wait_send()
            kv2z_copy(vg, 1, z, zz).wait_send()
            d2z_copy(z, zz).wait_send()

    @pl.when(y >= 2)
    def _():
        d2y_copy((y + 2) % NY).wait_send()

    @pl.when(y < 2)
    def _():
        kv2y_copy(kg, 0, y).wait_send()
        kv2y_copy(vg, 1, y).wait_send()

    for yrel in range(1, NY):
        for pair in range(PAIRS):
            slot_copy(yrel, pair).wait_send()
        t_copy(0, yrel).wait_send()
        t_copy(1, yrel).wait_send()

    for yrel in (1, 3):

        @pl.when(y + yrel < NY)
        def _():
            def kvy_sent(zz, carry):
                kvy_copy(kg, 0, y, yrel, zz).wait_send()
                kvy_copy(vg, 1, y, yrel, zz).wait_send()
                return carry

            lax.fori_loop(0, NZ, kvy_sent, 0)

        @pl.when(y >= yrel)
        def _():
            def dy_sent(blk, carry):
                dy_copy(yrel, y - yrel, blk).wait_send()
                return carry

            lax.fori_loop(0, PAIRS, dy_sent, 0)

    for h in range(2):
        core_copy(h).wait_send()
        for xrel in range(1, NX):
            xr_copy(h, xrel).wait_send()
            xg_copy(h, x, xrel).wait_send()
        for xx in range(NX):
            cg_copy(h, xx, c).wait_send()


def vmem(*shape, dtype=BF16):
    return pltpu.VMEM(shape, dtype)


def copy_kernel(*refs):
    for i in range(4):
        refs[4 + i][...] = refs[i][...]


def on_device(upper, ids, slots, probs, gate_pre, up_pre, w_gate, w_up, *rest):
    args = (upper, ids.T, slots.T, probs.T) + tuple(jnp.swapaxes(a, 1, 2) for a in (gate_pre, up_pre, w_gate, w_up)) + rest
    dma = pltpu.SemaphoreType.DMA
    whole = pl.BlockSpec(memory_space=pltpu.VMEM)
    anywhere = pl.BlockSpec(memory_space=pl.ANY)
    outs = [(TOK, COLS), (ATT, COLS), (ATT, HEAD_DIM), (ATT, HEAD_DIM)]
    out_shape = [jax.ShapeDtypeStruct(shape, BF16) for shape in outs]
    grads = pl.pallas_call(
        kernel,
        out_shape=out_shape,
        in_specs=[whole] * 4 + [anywhere] * 10,
        out_specs=[whole] * 4,
        scratch_shapes=[
            vmem(COLS, UNITS), vmem(COLS, UNITS), vmem(UNITS, COLS), vmem(UNITS, COLS),
            vmem(UNITS, COLS), vmem(UNITS, COLS), vmem(UNITS, COLS), vmem(ATT, COLS), vmem(ATT, COLS), vmem(ATT, COLS), dma((10,)),
            vmem(NZ, TOK, COLS), vmem(NZ, 8, 128, dtype=F32), vmem(8 * TOK, COLS), vmem(8 * TOK, ROW_SLOTS),
            vmem(PAIRS, 2 * TOK, ROW_SLOTS), vmem(NY, ROW_SLOTS, COLS), vmem(NY, ROW_SLOTS, COLS),
            vmem(2, ROW_SLOTS, UNITS, dtype=F32), vmem(2, ROW_SLOTS, UNITS), vmem(2, ROW_SLOTS, UNITS),
            vmem(2, NX, PAIR_SLOTS, UNITS), vmem(2, NX - 1, PAIR_SLOTS, UNITS), vmem(2, PAIR_SLOTS, UNITS, dtype=F32),
            vmem(2, NC, NX, PAIR_SLOTS, UNITS),
            vmem(NY, 2, PAIRS, PAIR_SLOTS, HALF_COLS), vmem(2, PAIRS, NY, PAIR_SLOTS, HALF_COLS),
            vmem(2, NZ, TOK, HALF_COLS), vmem(2, NZ, TOK, HALF_COLS), vmem(2, TOK, HALF_COLS, dtype=F32),
            vmem(NY * NZ, ATT, 128), vmem(NY * NZ, ATT, 128), vmem(ROWS, 128), vmem(ROWS, 128), vmem(1, ROWS, dtype=F32),
            vmem(BLOCKS, KEYS, ROWS, dtype=F32), vmem(8, ROWS, dtype=F32), vmem(8, ROWS, dtype=F32), vmem(1, ROWS, dtype=F32),
            vmem(128, ROWS, dtype=F32), vmem(NY * NZ, ATT, 256), vmem(NY - 1, NZ, ATT, 256), vmem(NZ, ATT, 256), vmem(ATT, 256), vmem(ATT, 256),
            vmem(NZ, ATT, 256), vmem(NZ, ATT, 256), vmem(ATT, 256, dtype=F32), vmem(ATT, 256, dtype=F32),
            dma((NZ,)), dma((NZ,)), dma((NZ,)), dma((NZ,)), dma((2, NZ)), dma((2, NZ)),
            dma((2, NY - 1, NZ)), dma((2, NY - 1, NZ)), dma((NY - 1, PAIRS)), dma((NY - 1, PAIRS)),
            dma((2,)), dma((2,)), dma((2, NX - 1)), dma((2, NX - 1)), dma((2, NX - 1)), dma((2, NX - 1)),
            dma((2, NX)), dma((2, NX)),
            dma((2, NY - 1)), dma((2, NY - 1)), dma((2, NZ)), dma((2, NZ)),
            dma((NY - 1, PAIRS)), dma((NY - 1, PAIRS)), dma((NZ,)), dma((NZ,)),
            dma((2,)), dma((2,)), dma((2, NZ)), dma((2, NZ)), dma((NZ,)), dma((NZ,)), dma((1,)), dma((1,)),
        ],
        compiler_params=pltpu.CompilerParams(
            collective_id=0, has_side_effects=True, vmem_limit_bytes=60 * 1024 * 1024
        ),
        cost_estimate=pl.CostEstimate(flops=9_000_000_000, bytes_accessed=14_000_000, transcendentals=8_000_000),
        name="layer_grad",
    )(*args)
    return pl.pallas_call(
        copy_kernel,
        out_shape=out_shape,
        in_specs=[whole] * 4,
        out_specs=[whole] * 4,
        name="hand_out",
    )(*grads)


def solution(mesh):
    return jax.shard_map(
        on_device,
        mesh=mesh,
        in_specs=(
            P("expert", "pipe"),
            P("expert", None),
            P("expert", None),
            P("expert", None),
            P("expert", None, None),
            P("expert", None, None),
            P("expert", "pipe", None),
            P("expert", "pipe", None),
            P("expert", None, "pipe"),
            P("expert", "pipe"),
            P("expert", "pipe"),
            P("expert", "pipe"),
            P("expert", "pipe"),
            P("expert", "pipe"),
        ),
        out_specs=(
            P("expert", "pipe"),
            P("expert", "pipe"),
            P("expert", "pipe"),
            P("expert", "pipe"),
        ),
        check_vma=False,
    )
```
